512 devices in a mesh: blk: 8 (over x, y_hi), tile: 64 (over z, y_lo, core).
Axes of the slice: x: 4, y: 8 (y_hi: 2, y_lo: 4; y = y_hi * 4 + y_lo), z: 8, core: 2. Of those that a mesh axis runs over, the one named last changes fastest.
Arguments:
- queries: bfloat16 [64, 2048, 768], P('tile', 'blk'), may hold values from -256 to 256
- key_rows: bfloat16 [64, 2048, 768], P('tile', 'blk'), may hold values from -256 to 256
- values: bfloat16 [64, 2048, 768], P('tile', 'blk'), may hold values from -6 to 6
- slide_lens: int32 [64], P('tile'), may hold values from 1024 to 2048, as said below
- sample_pos: int32 [64, 512], P('tile', 'blk'), may hold values from 0 to 255
- owner_ids: int32 [64, 512, 1], P('tile', 'blk'), may hold values from 0 to 63; in each aligned block of 64 rows (0 to 63, 64 to 127, ..., all dimensions but the last counted through in order) at most 2 rows name the same one
- owner_rows: int32 [64, 512], P('tile', 'blk'), may hold values from 0 to 15
- embed_proj: bfloat16 [1536, 768], P('tile'), may hold values from -0.21875 to 0.21875
- tile_states: bfloat16 [64, 128, 1536], P('tile'), may hold values from -40 to 40
- layernorm_gain: float32 [1536], replicated, may hold values from 0.1 to 1.9
- layernorm_bias: float32 [1536], replicated, may hold values from -3 to 3
- layer_scale: float32 [1536], replicated, may hold values from 0.2 to 2
- w_gate: bfloat16 [1536, 4096], P('tile', 'blk'), may hold values from -0.15625 to 0.15625
- w_up: bfloat16 [1536, 4096], P('tile', 'blk'), may hold values from -0.15625 to 0.15625
- w_down: bfloat16 [4096, 1536], P('blk', 'tile'), may hold values from -0.09375 to 0.09375
Outputs:
- state_grads: bfloat16 [64, 128, 1536], P('tile', 'blk')
The draws below stay inside these ranges and needn't reach their ends.
Inputs may be any that keep to these rules, and one draw needn't show every extreme that they name: `slide_lens`: at least one slide is full. `owner_ids`: at most 2 of the sampled tiles of one device go to one owner.
All inputs are finite; a program needn't handle non-finite values.
Results may differ from the reference program's by a relative error of at most 0.017.
Values may be sent and summed in bfloat16 or wider, within the bound.
A program may use at most 64 MiB of HBM per device.

```python
import math
import jax
import jax.numpy as jnp
import numpy as np
from jax import lax

D = 768
HEADS = 12
DT = 1536
FF = 4096
TOK_DEV = 256
SAMP_DEV = 64
OWN_DEV = 16
SEQ = 2048
SLIDES = 64
SAMPLES = 512
OWN_ROWS = 128
CAP = 2


STRENGTHS = (16.0, 24.0, 32.0)


def keys_common(key):
    base_key = jax.random.fold_in(key, 101)
    shape = (SLIDES, SEQ, D)
    gauss = jnp.clip(jax.random.normal(base_key, shape, jnp.float32), -4.0, 4.0)
    rows_all = gauss
    head_dim = D // HEADS
    head_rows = rows_all.reshape(SLIDES, SEQ, HEADS, head_dim)
    for index_pos, strength in enumerate(STRENGTHS):
        lead_row = head_rows[:, index_pos]
        head_rows = head_rows.at[:, index_pos].set(lead_row)
        near_row = head_rows[:, index_pos + 3]
        head_rows = head_rows.at[:, index_pos + 3].set(near_row)
    return head_rows.reshape(SLIDES, SEQ, D)


def queries_from(key):
    own_key = jax.random.fold_in(key, 2)
    shape = (SLIDES, SEQ, D)
    gauss = jnp.clip(jax.random.normal(own_key, shape, jnp.float32), -4.0, 4.0)
    rows_all = gauss
    for index_pos, strength in enumerate(STRENGTHS):
        target = SEQ - 1 - index_pos
        rows_all = rows_all.at[:, target].set(rows_all[:, target])
    return rows_all


def draw_key_rows(key, part):
    return keys_common(key).astype(jnp.bfloat16)


def draw_queries(key, part):
    return queries_from(key).astype(jnp.bfloat16)


def draw_slide_lens(key, part):
    key = jax.random.fold_in(key, 7)
    first_key, second_key = jax.random.split(key)
    lengths = jax.random.randint(first_key, (SLIDES,), SEQ // 2, SEQ + 1, dtype=jnp.int32)
    full_slot = jax.random.randint(second_key, (), 0, SLIDES, dtype=jnp.int32)
    return jnp.where(jnp.arange(SLIDES, dtype=jnp.int32) == full_slot, SEQ, lengths).astype(jnp.int32)


def states_from(key):
    split_keys = jax.random.split(key, 3)
    shape = (SLIDES, OWN_ROWS, DT)
    gauss = jnp.clip(jax.random.normal(split_keys[0], shape, jnp.float32), -4.0, 4.0)
    rows_all = gauss
    row_scale = jnp.exp(jax.random.uniform(split_keys[1], (SLIDES, OWN_ROWS, 1), jnp.float32, math.log(0.3), math.log(3.0)))
    column_scale = jnp.exp(jax.random.uniform(split_keys[2], (DT,), jnp.float32, math.log(0.3), math.log(3.0)))
    return rows_all * row_scale * column_scale


def draw_tile_states(key, part):
    key = jax.random.fold_in(key, 5)
    return states_from(key).astype(jnp.bfloat16)


def place_ends(result, rng, smallest, high):
    index_at = [jax.random.randint(jax.random.fold_in(rng, axis), (), 0, length) for axis, length in enumerate(result.shape)]
    longest = result.shape.index(max(result.shape))
    neighbour = index_at[:longest] + [(index_at[longest] + 1) % result.shape[longest]] + index_at[longest + 1:]
    return result.at[tuple(index_at)].set(smallest).at[tuple(neighbour)].set(high)


def levels(key, extent, cuts, low, largest):
    factor_of = 1.0
    for axis_at, shards_of in cuts:
        draws = jax.random.uniform(jax.random.fold_in(jax.random.fold_in(key, 6), axis_at), (shards_of,), jnp.float32, low / len(cuts), largest / len(cuts))
        factor_of = factor_of * jnp.repeat(jnp.exp(draws), extent[axis_at] // shards_of).reshape((-1,) + (1,) * (len(extent) - 1 - axis_at))
    return factor_of


def assign_block(stream_key, own, number, rows, count, top, limit, skew):
    ranking = jax.random.permutation(stream_key, count)
    crowded, usual = shares(count, rows * top, limit, skew, True), shares(count, rows * top, limit, skew, False)
    places = jnp.arange(count)

    def named(sizes, offset_by):
        used = int((sizes > 0).sum())
        fixed = max(1, used // 4)
        shifted = fixed + (places - fixed + offset_by * (used - fixed)) % max(1, count - fixed)
        return jnp.zeros((count,), jnp.int32).at[ranking[jnp.where(places < fixed, places, shifted)]].set(jnp.asarray(sizes, jnp.int32))

    sizes = jnp.where(number % 4 == 0, named(crowded, number // 4), named(usual, number - number // 4 - 1))
    mixed = jax.random.permutation(jax.random.fold_in(own, 3), count)
    giver, sink = mixed[0:count // 2 * 2:2], mixed[1:count // 2 * 2:2]
    slack = jnp.minimum(sizes[giver] - 1, limit - sizes[sink]) // 2
    slack = jnp.where((giver == ranking[0]) | (sink == ranking[0]) | (sizes[sink] == 0), 0, jnp.maximum(slack, 0))
    shifted = jax.random.randint(jax.random.fold_in(own, 4), (count // 2,), 0, 1 << 20) % (slack + 1)
    sizes = sizes.at[giver].add(-shifted).at[sink].add(shifted)
    labels = jnp.searchsorted(jnp.cumsum(sizes), jnp.arange(rows * top), side="right").astype(jnp.int32)
    grid = labels.reshape(top, rows).T
    grid = grid[jax.random.permutation(jax.random.fold_in(own, 1), rows)]
    offset_by = jax.random.randint(jax.random.fold_in(own, 2), (rows, 1), 0, top)
    return jnp.take_along_axis(grid, (jnp.arange(top)[None, :] + offset_by) % top, axis=1)


def shares(number_of, total, most, slope, full):
    loads = [(1 << 20) // math.isqrt(rank ** slope) + 1 for rank in range(1, number_of + 1)]
    largest = most if full else min(most, max(-(-total // number_of), total * loads[0] // sum(loads)))
    least = 1 if total - largest >= number_of - 1 else 0
    holding, spare = [largest] + [least] * (number_of - 1), total - largest - least * (number_of - 1)
    while spare > 0:
        movable = [i for i in range(1, number_of) if holding[i] < largest] or [i for i in range(1, number_of) if holding[i] < most]
        whole, left = sum([loads[i] for i in movable]), spare
        for i in movable:
            addition = min(most - holding[i], max(1, left * loads[i] // whole), spare)
            holding[i] = holding[i] + addition
            spare = spare - addition
    return np.array(holding)


def bell_draw(key, extent, deviation, most, cuts=(), kind=jnp.bfloat16):
    loudness = levels(key, extent, cuts, -0.22, 0.18) if cuts else 1.0
    drawn = jax.random.normal(key, extent, jnp.float32) * deviation * loudness
    return jnp.minimum(jnp.maximum(drawn, -most), most).astype(kind)


def setup_inputs(seed: int = 0) -> dict:
    key_list = jax.random.split(jax.random.key(seed), 16)
    queries = draw_queries(jax.random.fold_in(key_list[15], 71), 0)
    key_rows = draw_key_rows(jax.random.fold_in(key_list[15], 71), 0)
    values = bell_draw(key_list[2], (SLIDES, SEQ, D), 1.0, 6.0, ((0, 64), (1, 8)))
    slide_lens = draw_slide_lens(jax.random.fold_in(key_list[15], 71), 0)
    sample_pos = place_ends(jax.random.randint(key_list[4], (SLIDES, SAMPLES), 0, TOK_DEV), jax.random.fold_in(key_list[4], 1), 0, TOK_DEV - 1).astype(jnp.int32)
    owner_ids_keys = jax.random.split(jax.random.fold_in(key_list[5], 1), SLIDES * SAMPLES // SAMP_DEV)
    owner_ids_turns = jax.random.permutation(jax.random.fold_in(key_list[5], 3), SLIDES * SAMPLES // SAMP_DEV)
    owner_ids = jax.vmap(lambda own, number: assign_block(jax.random.fold_in(key_list[5], 2), own, number, SAMP_DEV, SLIDES, 1, CAP, 2))(owner_ids_keys, owner_ids_turns).reshape((SLIDES, SAMPLES, 1))
    owner_rows = place_ends(jax.random.randint(key_list[6], (SLIDES, SAMPLES), 0, OWN_DEV), jax.random.fold_in(key_list[6], 1), 0, OWN_DEV - 1).astype(jnp.int32)
    embed_proj = bell_draw(key_list[7], (DT, D), D ** -0.5, 0.21875, ((0, 64),))
    tile_states = draw_tile_states(jax.random.fold_in(key_list[15], 71), 0)
    layernorm_gain = jnp.clip(1.0 + 0.18 * jax.random.normal(key_list[9], (DT,), jnp.float32), 0.1, 1.9)
    layernorm_bias = bell_draw(key_list[10], (DT,), 0.5, 3.0, (), jnp.float32)
    layer_scale = jnp.clip(jnp.exp(jax.random.uniform(key_list[11], (DT,), jnp.float32, math.log(0.2), math.log(2.0))), 0.2, 2.0)
    w_gate = bell_draw(key_list[12], (DT, FF), DT ** -0.5, 0.15625, ((0, 64), (1, 8)))
    w_up = bell_draw(key_list[13], (DT, FF), DT ** -0.5, 0.15625, ((0, 64), (1, 8)))
    w_down = bell_draw(key_list[14], (FF, DT), FF ** -0.5, 0.09375, ((0, 8), (1, 64)))
    return dict(queries=queries, key_rows=key_rows, values=values, slide_lens=slide_lens, sample_pos=sample_pos, owner_ids=owner_ids, owner_rows=owner_rows, embed_proj=embed_proj, tile_states=tile_states, layernorm_gain=layernorm_gain, layernorm_bias=layernorm_bias, layer_scale=layer_scale, w_gate=w_gate, w_up=w_up, w_down=w_down)


def norm_components(hidden_state_values):
    mean_val = lax.optimization_barrier(jnp.mean(hidden_state_values, axis=-1, keepdims=True))
    centered = hidden_state_values - mean_val
    inverse_deviation = lax.rsqrt(lax.optimization_barrier(jnp.mean(centered * centered, axis=-1, keepdims=True)) + 1e-06)
    return (centered * inverse_deviation, inverse_deviation)

def reference(queries, key_rows, values, slide_lens, sample_pos, owner_ids, owner_rows, embed_proj, tile_states, layernorm_gain, layernorm_bias, layer_scale, w_gate, w_up, w_down):
    head_dim = D // HEADS
    scale_factor = 1.0 / math.sqrt(head_dim)

    def attend(inputs):
        query_rows, slide_keys, value_rows, length = inputs
        query_heads = query_rows.astype(jnp.float32).reshape(SEQ, HEADS, head_dim)
        key_heads = slide_keys.astype(jnp.float32).reshape(SEQ, HEADS, head_dim)
        value_heads = value_rows.astype(jnp.float32).reshape(SEQ, HEADS, head_dim)
        scores = jnp.einsum('qhd,khd->hqk', query_heads, key_heads) * scale_factor
        kept_keys = jnp.arange(SEQ, dtype=jnp.int32) < length
        scores = jnp.where(kept_keys[None, None, :], scores, -1e+30)
        row_top = lax.optimization_barrier(jnp.max(scores, axis=-1, keepdims=True))
        weights = jnp.where(kept_keys[None, None, :], jnp.exp(scores - row_top), 0.0)
        row_total = lax.optimization_barrier(jnp.sum(weights, axis=-1))
        rounded = weights.astype(jnp.bfloat16).astype(jnp.float32)
        mixed_rows = jnp.einsum('hqk,khd->qhd', rounded, value_heads)
        return (mixed_rows / row_total.T[:, :, None]).reshape(SEQ, D).astype(jnp.bfloat16)
    attended = lax.map(attend, (queries, key_rows, values, slide_lens))
    block_of = jnp.arange(SAMPLES, dtype=jnp.int32) // SAMP_DEV
    positions = sample_pos + (block_of * TOK_DEV)[None, :]
    picked = jax.vmap(lambda rows_in, index_in: jnp.take(rows_in, index_in, axis=0))(attended, positions)
    projected = jnp.einsum('snd,td->snt', picked.astype(jnp.float32), embed_proj.astype(jnp.float32))
    target = owner_ids[:, :, 0] * OWN_ROWS + block_of[None, :] * OWN_DEV + owner_rows
    table_grad = jax.ops.segment_sum(projected.reshape(-1, DT), target.reshape(-1).astype(jnp.int32), num_segments=SLIDES * OWN_ROWS)
    table_cot = table_grad.reshape(SLIDES, OWN_ROWS, DT).astype(jnp.bfloat16)

    def backward(inputs):
        hidden_state_values, incoming_gradients = inputs
        standardized_input, inverse_deviation = norm_components(hidden_state_values.astype(jnp.float32))
        normalized_rows = (standardized_input * layernorm_gain + layernorm_bias).astype(jnp.bfloat16)
        gate_proj = jnp.dot(normalized_rows, w_gate, preferred_element_type=jnp.float32)
        up_proj = jnp.dot(normalized_rows, w_up, preferred_element_type=jnp.float32)
        scaled = (incoming_gradients.astype(jnp.float32) * layer_scale).astype(jnp.bfloat16)
        hidden_cot = jnp.dot(scaled, w_down.T, preferred_element_type=jnp.float32)
        sigmoid_gate = jax.nn.sigmoid(gate_proj)
        gate_cot = (hidden_cot * up_proj * sigmoid_gate * (1.0 + gate_proj * (1.0 - sigmoid_gate))).astype(jnp.bfloat16)
        up_cot = (hidden_cot * gate_proj * sigmoid_gate).astype(jnp.bfloat16)
        normed_cot = jnp.dot(gate_cot, w_gate.T, preferred_element_type=jnp.float32) + jnp.dot(up_cot, w_up.T, preferred_element_type=jnp.float32)
        gain_scaled_gradient = normed_cot * layernorm_gain
        backward_output = incoming_gradients.astype(jnp.float32) + inverse_deviation * (gain_scaled_gradient - lax.optimization_barrier(jnp.mean(gain_scaled_gradient, axis=-1, keepdims=True)) - standardized_input * lax.optimization_barrier(jnp.mean(gain_scaled_gradient * standardized_input, axis=-1, keepdims=True)))
        return backward_output.astype(jnp.bfloat16)
    return lax.map(backward, (tile_states, table_cot))
```

```python
import functools
import math

import jax
import jax.numpy as jnp
from jax import lax
from jax.experimental import pallas as pl
from jax.experimental.pallas import tpu as pltpu
from jax.sharding import PartitionSpec as P

X, YH = 4, 2
Z, YL, CORES = 8, 4, 2
HEAD_DIM = 64
CAP = 2
EPS = 1e-06
NEG = -1e30
FLOOR = -1e29
STATS = 48
F32, BF16 = jnp.float32, jnp.bfloat16
MESH = pl.DeviceIdType.MESH

NT = (((1,), (1,)), ((), ()))
NN = (((1,), (0,)), ((), ()))


def dot(a, b, dims=NN):
    return lax.dot_general(a, b, dims, preferred_element_type=F32)


def iota(shape, axis):
    return lax.broadcasted_iota(jnp.int32, shape, axis)


def as_column(row):
    n = row.shape[1]
    same = iota((n, n), 0) == iota((n, n), 1)
    return jnp.sum(jnp.where(same, row, 0), axis=1, keepdims=True)


def split3(value):
    high = value.astype(BF16).astype(F32)
    rest = value - high
    middle = rest.astype(BF16).astype(F32)
    return high, middle, rest - middle


def standardize(rows):
    centered = rows - jnp.mean(rows, axis=-1, keepdims=True)
    inverse = lax.rsqrt(jnp.mean(centered * centered, axis=-1, keepdims=True) + EPS)
    return centered * inverse, inverse


def kernel(
    len_ref, q_ref, k_ref, v_ref, pos_ref, own_ref, row_ref, e_ref, st_ref,
    gain_ref, bias_ref, ls_ref, wg_ref, wu_ref, wd_ref,
    out_ref,
    qall, vt, mask, stat, ret, ret_in, ysend, ymine, yrecv,
    xs, r1, x2, r2, cot, cot_sum, rs, rs_in, ry_send, ry_in,
    wpair, wout, wfull, normed, fwd, hid, gu,
    send_sems, recv_sems,
):
    blk, tile = lax.axis_index("blk"), lax.axis_index("tile")
    x, yh = blk // YH, blk % YH
    core = tile % CORES
    yl = (tile // CORES) % YL
    z = tile // (CORES * YL)
    lane = tile % (CORES * YL)
    side = CORES * YL

    tokens, width = k_ref.shape[1], k_ref.shape[2]
    samples = pos_ref.shape[1]
    both = YH * samples
    heads_half = width // HEAD_DIM // 2
    half_rows = width // 2
    ff = wg_ref.shape[1]
    own = out_ref.shape[1]
    rows_all = st_ref.shape[1]
    dt = st_ref.shape[2]
    shard = e_ref.shape[0]
    scale = 1.0 / math.sqrt(HEAD_DIM) * math.log2(math.e)
    e_a = (width - ff) // 2

    def at(new_x=None, new_yh=None, new_z=None, new_yl=None, new_core=None):
        a = x if new_x is None else new_x
        b = yh if new_yh is None else new_yh
        c = z if new_z is None else new_z
        d = yl if new_yl is None else new_yl
        e = core if new_core is None else new_core
        return (a * YH + b, (c * YL + d) * CORES + e)

    def x_peer(d):
        return at(new_x=lax.rem(x + d, X))

    def z_peer(d):
        return at(new_z=lax.rem(z + d + Z, Z))

    def side_peer(d):
        other = lax.rem(lane + d, side)
        return (blk, z * side + other)

    partner = at(new_yh=1 - yh)
    sibling = at(new_core=1 - core)

    copies = []

    def send(src, dst, target):
        index = len(copies)
        copy = pltpu.make_async_remote_copy(
            src_ref=src, dst_ref=dst,
            send_sem=send_sems.at[index], recv_sem=recv_sems.at[index],
            device_id=target, device_id_type=MESH,
        )
        copy.start()
        copies.append(copy)
        return copy

    barrier = pltpu.get_barrier_semaphore()
    targets = [partner]
    targets += [x_peer(d) for d in range(1, X)]
    targets += [z_peer(d) for d in range(1, Z)]
    targets += [side_peer(d) for d in range(1, side)]
    for target in targets:
        pl.semaphore_signal(barrier, inc=1, device_id=target, device_id_type=MESH)

    chosen = (as_column(pos_ref[...]) == iota((samples, tokens), 1)).astype(F32).astype(BF16)
    my_rows = pl.ds(pl.multiple_of(yh * samples, samples), samples)
    qall[x, my_rows, :] = dot(chosen, q_ref[0]).astype(BF16)


    def fill(mine, first):
        if first:
            mine[:, 0:ff] = wg_ref[...]
            mine[:, ff:2 * ff] = wu_ref[...]
            mine[:, 2 * ff:] = e_ref[:, 0:e_a]
        else:
            mine[:, 0:ff] = wd_ref[...]
            mine[:, ff:] = e_ref[:, e_a:]

    @pl.when(core == 0)
    def _():
        fill(wpair.at[0], True)
        fill(wout, False)

    @pl.when(core == 1)
    def _():
        fill(wpair.at[1], False)
        fill(wout, True)

    pl.semaphore_wait(barrier, len(targets))

    q_y = send(qall.at[x, my_rows], qall.at[x, my_rows], partner)
    w_pair = send(wout, wpair.at[core], sibling)

    positions = blk * tokens + iota((tokens, 2 * both), 0)
    mask[...] = jnp.where(positions < len_ref[0], 0.0, NEG).astype(F32)
    vt[...] = v_ref[0].astype(F32).T.astype(BF16)
    stat[...] = jnp.zeros_like(stat)

    w_pair.wait_recv()
    wfull[core, z, yl] = jnp.concatenate(
        [wpair[0].astype(F32), wpair[1].astype(F32)], axis=0
    ).astype(BF16)
    w_line = [
        send(
            wfull.at[core, z, yl], wfull.at[core, z, yl],
            at(new_yl=lax.rem(yl + d, YL)),
        )
        for d in range(1, YL)
    ]

    q_y.wait_recv()
    q_x = {d: send(qall.at[x], qall.at[x], x_peer(d)) for d in (1, 3, 2) if d < X}

    for copy in w_line:
        copy.wait_recv()

    ring, pass_on = {}, []
    cut = YL // 2

    def on_ring(step):
        up, down = lax.rem(z - (step - 1) + Z, Z), lax.rem(z + (step - 1), Z)
        if step < Z // 2:
            ring[step] = (
                send(wfull.at[core, up], wfull.at[core, up], z_peer(1)),
                send(wfull.at[core, down], wfull.at[core, down], z_peer(-1)),
            )
        else:
            first, second = pl.ds(0, cut), pl.ds(cut, YL - cut)
            ring[step] = (
                send(wfull.at[core, up, first], wfull.at[core, up, first], z_peer(1)),
                send(wfull.at[core, down, second], wfull.at[core, down, second], z_peer(-1)),
            )

    def to_sibling(block):
        pass_on.append(send(wfull.at[core, block], wfull.at[core, block], sibling))

    def arrived(step):
        for copy in ring[step]:
            copy.wait_recv()
        if step < Z // 2:
            on_ring(step + 1)
            to_sibling(lax.rem(z - step + Z, Z))
            to_sibling(lax.rem(z + step, Z))
        else:
            to_sibling(lax.rem(z + step, Z))

    def attend(block):
        def one_half(half, carry):
            for pair in range(heads_half // 2):
                start = pl.multiple_of(half * half_rows + pair * 128, 128)
                features = pl.ds(start, 128)
                wide = qall[block, :, features]
                low = iota((both, 128), 1) < HEAD_DIM
                zero = jnp.zeros_like(wide)
                queries = jnp.concatenate(
                    [jnp.where(low, wide, zero), jnp.where(low, zero, wide)], axis=0
                )
                scores = dot(k_ref[0, :, features], queries, NT) + mask[...]
                top = jnp.maximum(jnp.max(scores, axis=0, keepdims=True), FLOOR)
                weights = jnp.exp2((scores - top) * scale)
                total = jnp.sum(weights, axis=0, keepdims=True)
                mixed = dot(vt[features, :], weights.astype(BF16))
                for j in range(2):
                    head = 2 * pair + j
                    here = slice(j * both, (j + 1) * both)
                    ret[block, half, head * 64:head * 64 + 64, :] = mixed[
                        j * 64:j * 64 + 64, here
                    ].astype(BF16)
                    stat[0, head:head + 1, :] = top[:, here]
                    stat[1, head:head + 1, :] = total[:, here]
            tops = split3(stat[0])
            totals = split3(stat[1])
            pieces = tops + totals[:2] + (jnp.zeros_like(tops[0]),)
            ret[block, half, half_rows:, :] = jnp.concatenate(pieces, axis=0).astype(BF16)
            return carry

        lax.fori_loop(0, 2, one_half, 0)

    def merge(parts):
        stats = [part[half_rows:] for part in parts]
        tops = [s[0:8] + s[8:16] + s[16:24] for s in stats]
        top = functools.reduce(jnp.maximum, tops)
        factors = [jnp.exp2((t - top) * scale) for t in tops]
        total = sum(f * (s[24:32] + s[32:40]) for f, s in zip(factors, stats))
        rows = []
        for head in range(heads_half):
            here = slice(head * 64, head * 64 + 64)
            rows.append(sum(f[head:head + 1] * p[here] for f, p in zip(factors, parts)))
        return rows, top, total

    on_ring(1)
    to_sibling(z)
    attend(x)

    xhat, unused = standardize(st_ref[0].astype(F32))
    gain = gain_ref[...].reshape(1, dt)
    normed[...] = (xhat * gain + bias_ref[...].reshape(1, dt)).astype(BF16)

    arrived(1)

    back = {}
    for position, d in enumerate(d for d in (1, 3, 2) if d < X):
        q_x[d].wait_recv()
        block = lax.rem(x - d + X, X)
        attend(block)
        back[d] = send(ret.at[block], ret_in.at[X - d - 1], at(new_x=block))
        if position == 1:
            arrived(2)
    for step in range(2 if X < 3 else 3, Z // 2):
        arrived(step)

    for d in back:
        back[d].wait_recv()
    for half in range(2):
        rows, top, total = merge(
            [ret[x, half].astype(F32)] + [ret_in[d, half].astype(F32) for d in range(X - 1)]
        )
        tops, totals = split3(top), split3(total)
        ymine[half] = jnp.concatenate(
            rows + list(tops) + list(totals[:2]) + [jnp.zeros_like(top)], axis=0
        )

    low = iota((half_rows + STATS, both), 1) < samples
    first, second = ymine[0], ymine[1]
    for_low = jnp.where(low, first, pltpu.roll(second, samples, 1))
    for_high = jnp.where(low, pltpu.roll(first, samples, 1), second)

    @pl.when(yh == 0)
    def _():
        ysend[...] = for_high.astype(BF16)
        ymine[0] = for_low

    @pl.when(yh == 1)
    def _():
        ysend[...] = for_low.astype(BF16)
        ymine[0] = for_high

    back_y = send(ysend, yrecv, partner)

    slots = Z * side * CAP
    owner_row = own_ref[...]
    owner_col = as_column(owner_row)
    square = (samples, samples)
    earlier = (owner_col == owner_row) & (iota(square, 0) < iota(square, 1))
    rank = jnp.sum(jnp.where(earlier, 1, 0), axis=0, keepdims=True)
    slot = owner_row * CAP + rank
    hit = iota((slots, samples), 0) == slot
    table_row = jnp.sum(jnp.where(hit, row_ref[...] + 1, 0), axis=1, keepdims=True) - 1
    xs[:, width:] = (table_row == iota((slots, 128), 1)).astype(F32).astype(BF16)
    hit = hit.astype(F32)
    none = jnp.zeros_like(hit)
    spread = jnp.concatenate(
        [jnp.concatenate([hit, none], axis=1), jnp.concatenate([none, hit], axis=1)], axis=0
    ).astype(BF16)

    back_y.wait_recv()
    rows, unused, total = merge([ymine[0], yrecv[...].astype(F32)])
    picked = jnp.concatenate(
        [rows[h] / total[h:h + 1] for h in range(heads_half)], axis=0
    ).astype(BF16)
    placed = dot(spread, picked, NT).astype(BF16)
    xs[:, 0:half_rows] = placed[0:slots]
    xs[:, half_rows:width] = placed[slots:]

    group = side * CAP

    def rows_of(index):
        return pl.ds(pl.multiple_of(index * group, group), group)

    along_z = [
        send(xs.at[rows_of(lax.rem(z + d, Z))], r1.at[z], z_peer(d)) for d in range(1, Z)
    ]
    r1[z] = xs[rows_of(z), :]
    arrived(Z // 2)

    count = Z * CAP
    for copy in along_z:
        copy.wait_recv()
    to_row, from_row = iota((slots, slots), 0), iota((slots, slots), 1)
    wanted = ((to_row // CAP) % Z) * group + (to_row // count) * CAP + to_row % CAP
    order = (wanted == from_row).astype(F32).astype(BF16)
    x2[...] = dot(order, r1[...].reshape(slots, width + 128)).astype(BF16)

    def owner_rows_of(index):
        return pl.ds(pl.multiple_of(index * count, count), count)

    along_side = [
        send(x2.at[owner_rows_of(lax.rem(lane + d, side))], r2.at[lane], side_peer(d))
        for d in range(1, side)
    ]
    r2[lane] = x2[owner_rows_of(lane), :]

    for copy in pass_on:
        copy.wait_recv()

    step_rows = 2 * YL * CORES * shard
    steps = dt // step_rows

    def block_of(half, i, columns):
        return wfull[half, pl.ds(2 * i, 2), :, :, columns].reshape(
            step_rows, columns.stop - columns.start
        )

    def columns_of(i):
        return pl.ds(pl.multiple_of(i * step_rows, step_rows), step_rows)

    fwd[...] = jnp.zeros_like(fwd)

    def forward(i, carry):
        fwd[...] += dot(normed[:, columns_of(i)], block_of(0, i, slice(0, 2 * ff)))
        return carry

    lax.fori_loop(0, steps, forward, 0)

    for copy in along_side:
        copy.wait_recv()
    got = r2[...].reshape(slots, width + 128)
    combine = got[:, width:].astype(F32).T[0:own].astype(BF16)
    grad = dot(combine, got[:, 0:width])
    grad_high = grad.astype(BF16)
    grad_low = (grad - grad_high.astype(F32)).astype(BF16)
    grads = jnp.concatenate([grad_high.astype(F32), grad_low.astype(F32)], axis=0).astype(BF16)

    my_table = pl.ds(pl.multiple_of(yh * own, own), own)

    def project(i, carry):
        terms = dot(grads[:, 0:e_a], block_of(0, i, slice(2 * ff, 2 * ff + e_a)), NT)
        terms += dot(grads[:, e_a:], block_of(1, i, slice(ff, ff + width - e_a)), NT)
        cot_sum[:, columns_of(i)] = terms[0:own] + terms[own:]
        return carry

    lax.fori_loop(0, steps, project, 0)
    cot[x, my_table, :] = cot_sum[...].astype(BF16)
    cot_y = send(cot.at[x, my_table], cot.at[x, my_table], partner)
    cot_y.wait_recv()
    cot_x = [send(cot.at[x], cot.at[x], x_peer(d)) for d in range(1, X)]
    for copy in cot_x:
        copy.wait_recv()

    layer_scale = ls_ref[...].reshape(1, dt)
    scaled = (cot[...].reshape(rows_all, dt).astype(F32) * layer_scale).astype(BF16)
    normed[...] = scaled
    hid[...] = jnp.zeros_like(hid)

    def hidden(i, carry):
        hid[...] += dot(normed[:, columns_of(i)], block_of(1, i, slice(0, ff)))
        return carry

    lax.fori_loop(0, steps, hidden, 0)
    gate, up, hidden_cot = fwd[:, 0:ff], fwd[:, ff:], hid[...]
    sigmoid = jax.nn.sigmoid(gate)
    gu[:, 0:ff] = (hidden_cot * up * sigmoid * (1.0 + gate * (1.0 - sigmoid))).astype(BF16)
    gu[:, ff:] = (hidden_cot * gate * sigmoid).astype(BF16)

    def backward(i, carry):
        terms = dot(gu[...], block_of(0, i, slice(0, 2 * ff)), NT)
        rs[:, :, columns_of(i)] = terms.astype(BF16).reshape(X, YH * own, step_rows)
        return carry

    lax.fori_loop(0, steps, backward, 0)
    sum_x = [
        send(rs.at[lax.rem(x + d, X)], rs_in.at[d - 1], x_peer(d)) for d in range(1, X)
    ]

    xhat, inverse = standardize(
        st_ref[0, pl.ds(pl.multiple_of(blk * own, own), own), :].astype(F32)
    )
    for copy in sum_x:
        copy.wait_recv()
    partial = rs[x].astype(F32)
    for d in range(X - 1):
        partial += rs_in[d].astype(F32)

    @pl.when(yh == 0)
    def _():
        ry_send[...] = partial[own:].astype(BF16)
        cot_sum[...] = partial[0:own]

    @pl.when(yh == 1)
    def _():
        ry_send[...] = partial[0:own].astype(BF16)
        cot_sum[...] = partial[own:]

    sum_y = send(ry_send, ry_in, partner)
    sum_y.wait_recv()
    grads_in = (cot_sum[...] + ry_in[...].astype(F32)) * gain
    result = cot[x, my_table, :].astype(F32) + inverse * (
        grads_in
        - jnp.mean(grads_in, axis=-1, keepdims=True)
        - xhat * jnp.mean(grads_in * xhat, axis=-1, keepdims=True)
    )
    out_ref[0] = result.astype(BF16)

    for copy in copies:
        copy.wait_send()


def local(
    queries, key_rows, values, slide_lens, sample_pos, owner_ids, owner_rows, embed_proj,
    tile_states, layernorm_gain, layernorm_bias, layer_scale, w_gate, w_up, w_down,
):
    tokens, width = key_rows.shape[1:]
    samples = sample_pos.shape[1]
    rows_all, dt = tile_states.shape[1:]
    shard, ff = w_gate.shape
    own = rows_all // (X * YH)
    both = YH * samples
    half_all = width // 2 + STATS
    side = CORES * YL
    slots = Z * side * CAP
    part = (3 * ff + width) // 2
    vmem = pltpu.VMEM
    scratch = [
        vmem((X, both, width), BF16),
        vmem((width, tokens), BF16),
        vmem((tokens, 2 * both), F32),
        vmem((2, 8, both), F32),
        vmem((X, 2, half_all, both), BF16),
        vmem((X - 1, 2, half_all, both), BF16),
        vmem((half_all, both), BF16),
        vmem((2, half_all, both), F32),
        vmem((half_all, both), BF16),
        vmem((slots, width + 128), BF16),
        vmem((Z, side * CAP, width + 128), BF16),
        vmem((slots, width + 128), BF16),
        vmem((side, Z * CAP, width + 128), BF16),
        vmem((X, YH * own, dt), BF16),
        vmem((own, dt), F32),
        vmem((X, YH * own, dt), BF16),
        vmem((X - 1, YH * own, dt), BF16),
        vmem((own, dt), BF16),
        vmem((own, dt), BF16),
        vmem((CORES, shard, part), BF16),
        vmem((shard, part), BF16),
        vmem((2, Z, YL, CORES * shard, part), BF16),
        vmem((rows_all, dt), BF16),
        vmem((rows_all, 2 * ff), F32),
        vmem((rows_all, ff), F32),
        vmem((rows_all, 2 * ff), BF16),
        pltpu.SemaphoreType.DMA((64,)),
        pltpu.SemaphoreType.DMA((64,)),
    ]
    in_vmem = pl.BlockSpec(memory_space=pltpu.VMEM)
    return pl.pallas_call(
        kernel,
        out_shape=jax.ShapeDtypeStruct((1, own, dt), BF16),
        in_specs=[pl.BlockSpec(memory_space=pltpu.SMEM)] + [in_vmem] * 14,
        out_specs=in_vmem,
        scratch_shapes=scratch,
        compiler_params=pltpu.CompilerParams(
            collective_id=0, has_side_effects=True, vmem_limit_bytes=40 * 1024 * 1024
        ),
    )(
        slide_lens, queries, key_rows, values, sample_pos, owner_ids[:, :, 0], owner_rows,
        embed_proj, tile_states, layernorm_gain, layernorm_bias, layer_scale, w_gate, w_up,
        w_down.T,
    )


def solution(mesh):
    return jax.shard_map(
        local,
        mesh=mesh,
        in_specs=(
            P("tile", "blk", None),
            P("tile", "blk", None),
            P("tile", "blk", None),
            P("tile"),
            P("tile", "blk"),
            P("tile", "blk", None),
            P("tile", "blk"),
            P("tile", None),
            P("tile", None, None),
            P(),
            P(),
            P(),
            P("tile", "blk"),
            P("tile", "blk"),
            P("blk", "tile"),
        ),
        out_specs=P("tile", "blk", None),
        check_vma=False,
    )
```

```python
import functools
import math

import jax
import jax.numpy as jnp
from jax import lax
from jax.experimental import pallas as pl
from jax.experimental.pallas import tpu as pltpu
from jax.sharding import PartitionSpec as P

X, YH = 4, 2
Z, YL, CORES = 8, 4, 2
HEAD_DIM = 64
CAP = 2
EPS = 1e-06
NEG = -1e30
FLOOR = -1e29
STATS = 48
F32, BF16 = jnp.float32, jnp.bfloat16
MESH = pl.DeviceIdType.MESH

NT = (((1,), (1,)), ((), ()))
NN = (((1,), (0,)), ((), ()))


def dot(a, b, dims=NN):
    return lax.dot_general(a, b, dims, preferred_element_type=F32)


def iota(shape, axis):
    return lax.broadcasted_iota(jnp.int32, shape, axis)


def as_column(row):
    n = row.shape[1]
    same = iota((n, n), 0) == iota((n, n), 1)
    return jnp.sum(jnp.where(same, row, 0), axis=1, keepdims=True)


def split3(value):
    high = value.astype(BF16).astype(F32)
    rest = value - high
    middle = rest.astype(BF16).astype(F32)
    return high, middle, rest - middle


def standardize(rows):
    centered = rows - jnp.mean(rows, axis=-1, keepdims=True)
    inverse = lax.rsqrt(jnp.mean(centered * centered, axis=-1, keepdims=True) + EPS)
    return centered * inverse, inverse


def kernel(
    len_hbm, q_hbm, k_hbm, v_hbm, pos_hbm, own_hbm, row_hbm, e_hbm, st_hbm,
    gain_hbm, bias_hbm, ls_hbm, wg_hbm, wu_hbm, wd_hbm,
    out_ref,
    len_ref, q_ref, k_ref, v_ref, pos_ref, own_ref, row_ref, e_ref, st_ref,
    gain_ref, bias_ref, ls_ref, wg_ref, wu_ref, wd_ref,
    qall, kmask, vt, mask, stat, ret, ret_in, ysend, ymine, yrecv,
    xs, r1, x2, r2, cot, cot_sum, rs, rs_in, ry_send, ry_in,
    wpair, wout, wfull, efull, normed, fwd, hid, gu,
    load_sems, send_sems, recv_sems,
):
    blk, tile = lax.axis_index("blk"), lax.axis_index("tile")
    x, yh = blk // YH, blk % YH
    core = tile % CORES
    yl = (tile // CORES) % YL
    z = tile // (CORES * YL)
    lane = tile % (CORES * YL)
    side = CORES * YL

    tokens, width = k_ref.shape[1], k_ref.shape[2]
    samples = pos_ref.shape[1]
    heads_half = width // HEAD_DIM // 2
    half_rows = width // 2
    ff = wg_ref.shape[1]
    own = out_ref.shape[1]
    rows_all = st_ref.shape[1]
    dt = st_ref.shape[2]
    shard = e_ref.shape[0]
    scale = 1.0 / math.sqrt(HEAD_DIM) * math.log2(math.e)
    part = 3 * ff // 2

    def at(new_x=None, new_yh=None, new_z=None, new_yl=None, new_core=None):
        a = x if new_x is None else new_x
        b = yh if new_yh is None else new_yh
        c = z if new_z is None else new_z
        d = yl if new_yl is None else new_yl
        e = core if new_core is None else new_core
        return (a * YH + b, (c * YL + d) * CORES + e)

    def x_peer(d):
        return at(new_x=lax.rem(x + d, X))

    def z_peer(d):
        return at(new_z=lax.rem(z + d + Z, Z))

    def side_peer(d):
        other = lax.rem(lane + d, side)
        return (blk, z * side + other)

    def y_peer(d):
        place = lax.rem(yh * YL + yl + d + YH * YL, YH * YL)
        return at(new_yh=place // YL, new_yl=place % YL)

    partner = at(new_yh=1 - yh)
    sibling = at(new_core=1 - core)

    loads = {}
    for index, (name, source, target) in enumerate([
        ("pos", pos_hbm, pos_ref), ("q", q_hbm, q_ref), ("wg", wg_hbm, wg_ref),
        ("wu", wu_hbm, wu_ref), ("wd", wd_hbm, wd_ref), ("e", e_hbm, e_ref),
        ("len", len_hbm, len_ref), ("k", k_hbm, k_ref), ("v", v_hbm, v_ref),
        ("st", st_hbm, st_ref), ("gain", gain_hbm, gain_ref), ("bias", bias_hbm, bias_ref),
        ("own", own_hbm, own_ref), ("row", row_hbm, row_ref), ("ls", ls_hbm, ls_ref),
    ]):
        loads[name] = pltpu.make_async_copy(source, target, load_sems.at[index])
        loads[name].start()

    def loaded(*names):
        for name in names:
            loads.pop(name).wait()

    copies = []

    def send(src, dst, target):
        index = len(copies)
        copy = pltpu.make_async_remote_copy(
            src_ref=src, dst_ref=dst,
            send_sem=send_sems.at[index], recv_sem=recv_sems.at[index],
            device_id=target, device_id_type=MESH,
        )
        copy.start()
        copies.append(copy)
        return copy

    barrier = pltpu.get_barrier_semaphore()
    targets = [partner]
    targets += [x_peer(d) for d in range(1, X)]
    targets += [z_peer(d) for d in range(1, Z)]
    targets += [side_peer(d) for d in range(1, side)]
    targets += [y_peer(d) for d in (1, -1, 2, -2)]
    for target in targets:
        pl.semaphore_signal(barrier, inc=1, device_id=target, device_id_type=MESH)

    loaded("pos", "q")
    chosen = (as_column(pos_ref[...]) == iota((samples, tokens), 1)).astype(F32).astype(BF16)
    my_rows = pl.ds(pl.multiple_of(x * samples, samples), samples)
    qall[yh, my_rows, :] = dot(chosen, q_ref[0]).astype(BF16)

    loaded("wg", "wu", "wd", "e")
    cut = ff // 2

    def fill(mine, first):
        if first:
            mine[:, 0:ff] = wg_ref[...]
            mine[:, ff:part] = wu_ref[:, 0:cut]
            mine[:, part:] = e_ref[:, 0:half_rows]
        else:
            mine[:, 0:cut] = wu_ref[:, cut:]
            mine[:, cut:part] = wd_ref[...]
            mine[:, part:] = e_ref[:, half_rows:]

    @pl.when(core == 0)
    def _():
        fill(wpair.at[0], True)
        fill(wout, False)

    @pl.when(core == 1)
    def _():
        fill(wpair.at[1], False)
        fill(wout, True)

    pl.semaphore_wait(barrier, len(targets))

    def to_x_peers(group):
        rows = qall.at[group, my_rows]
        return {d: send(rows, rows, x_peer(d)) for d in range(1, X)}

    q_y = send(qall.at[yh, my_rows], qall.at[yh, my_rows], partner)
    w_pair = send(wout, wpair.at[core], sibling)
    q_near = to_x_peers(yh)

    loaded("len", "k", "v")
    positions = blk * tokens + iota((tokens, X * samples), 0)
    mask[...] = jnp.where(positions < len_ref[0], 0.0, NEG).astype(F32)
    vt[...] = v_ref[0].astype(F32).T.astype(BF16)
    keys = k_ref[0]
    even = iota((tokens, width), 1) % 128 < HEAD_DIM
    kmask[0] = jnp.where(even, keys, jnp.zeros_like(keys))
    kmask[1] = jnp.where(even, jnp.zeros_like(keys), keys)
    stat[...] = jnp.zeros_like(stat)

    w_pair.wait_recv()
    whole = jnp.concatenate([wpair[0].astype(F32), wpair[1].astype(F32)], axis=0).astype(BF16)
    wfull[core, z, yl] = whole[:, 0:part]
    efull[core, z, yl] = whole[:, part:]

    turn = 1 - 2 * core

    def step_blocks(step):
        up, down = lax.rem(z - (step - 1) + Z, Z), lax.rem(z + (step - 1), Z)
        if step < Z // 2:
            return [(up, 1), (down, -1)]
        return [(lax.rem(z - turn * (step - 1) + Z, Z), turn)]

    def first_ring(step):
        return [
            send(ref.at[core, block, yl], ref.at[core, block, yl], z_peer(way))
            for block, way in step_blocks(step)
            for ref in (efull, wfull)
        ]

    def second_ring(step):
        sent = []
        for block, way in step_blocks(step):
            for d in range(1, YL):
                place = wfull.at[core, block, lax.rem(yl + d, YL)]
                sent.append(send(place, place, z_peer(way)))
        return sent

    e_line = []

    def e_along_y(block, way):
        place = efull.at[core, block, yl]
        for d in (1, -1, 2 * way):
            e_line.append(send(place, place, y_peer(d)))

    def wait(sent):
        for copy in sent:
            copy.wait_recv()

    pass_on = []

    def to_sibling(block):
        pass_on.append(send(wfull.at[core, block], wfull.at[core, block], sibling))

    def arrived_first(sent, step):
        wait(sent)
        following = None
        if step < Z // 2:
            following = first_ring(step + 1)
            e_along_y(lax.rem(z - step + Z, Z), 1)
            e_along_y(lax.rem(z + step, Z), -1)
        else:
            e_along_y(lax.rem(z + step, Z), 1)
        return following

    def arrived_second(sent, step):
        wait(sent)
        following = None
        if step < Z // 2:
            following = second_ring(step + 1)
            to_sibling(lax.rem(z - step + Z, Z))
        to_sibling(lax.rem(z + step, Z))
        return following

    ring = first_ring(1)
    e_along_y(z, 1)

    loaded("st", "gain", "bias")
    xhat, unused = standardize(st_ref[0].astype(F32))
    gain = gain_ref[...].reshape(1, dt)
    normed[...] = (xhat * gain + bias_ref[...].reshape(1, dt)).astype(BF16)

    ring = arrived_first(ring, 1)

    q_y.wait_recv()
    q_far = to_x_peers(1 - yh)
    w_line = [
        send(
            wfull.at[core, z, yl], wfull.at[core, z, yl],
            at(new_yl=lax.rem(yl + d, YL)),
        )
        for d in range(1, YL)
    ]

    def pack(first, second):
        both = 2 * samples
        low = iota((first.shape[0], both), 1) < samples
        pieces = []
        for start in range(0, X * samples, both):
            a, b = first[:, start:start + both], second[:, start:start + both]
            pieces.append(jnp.where(low, a, pltpu.roll(b, samples, 1)))
            pieces.append(jnp.where(low, pltpu.roll(a, samples, 1), b))
        return pieces

    def attend(group):
        def two_pairs(j, carry):
            for parity in range(2):
                head = 2 * j + parity
                mixed = []
                for half in range(2):
                    start = pl.multiple_of(half * half_rows + j * 128, 128)
                    features = pl.ds(start, 128)
                    scores = dot(kmask[parity, :, features], qall[group, :, features], NT)
                    scores += mask[...]
                    top = jnp.maximum(jnp.max(scores, axis=0, keepdims=True), FLOOR)
                    weights = jnp.exp2((scores - top) * scale)
                    stat[half, 0, pl.ds(head, 1), :] = top
                    stat[half, 1, pl.ds(head, 1), :] = jnp.sum(weights, axis=0, keepdims=True)
                    mine = pl.ds(pl.multiple_of(start + parity * 64, 64), 64)
                    mixed.append(dot(vt[mine, :], weights.astype(BF16)))
                rows = pl.ds(pl.multiple_of(head * 64, 64), 64)
                for place, piece in enumerate(pack(*mixed)):
                    ret[group, place, rows, :] = piece.astype(BF16)
            return carry

        lax.fori_loop(0, heads_half // 2, two_pairs, 0)
        tops, totals = pack(stat[0, 0], stat[1, 0]), pack(stat[0, 1], stat[1, 1])
        for place in range(X):
            pieces = split3(tops[place]) + split3(totals[place])[:2]
            pieces += (jnp.zeros_like(pieces[0]),)
            ret[group, place, half_rows:, :] = jnp.concatenate(pieces, axis=0).astype(BF16)

    def back_to_x_peers(group):
        sent = []
        for d in range(1, X):
            place = lax.rem(x + d, X)
            sent.append(send(ret.at[group, place], ret_in.at[group, d - 1], x_peer(d)))
        return sent

    def merge(parts):
        stats = [piece[half_rows:] for piece in parts]
        tops = [s[0:8] + s[8:16] + s[16:24] for s in stats]
        top = functools.reduce(jnp.maximum, tops)
        factors = [jnp.exp2((t - top) * scale) for t in tops]
        total = sum(f * (s[24:32] + s[32:40]) for f, s in zip(factors, stats))
        rows = []
        for head in range(heads_half):
            here = slice(head * 64, head * 64 + 64)
            rows.append(sum(f[head:head + 1] * p[here] for f, p in zip(factors, parts)))
        return rows, top, total

    def merged(group):
        rows, top, total = merge(
            [ret[group, x].astype(F32)]
            + [ret_in[group, d].astype(F32) for d in range(X - 1)]
        )
        pieces = split3(top) + split3(total)[:2] + (jnp.zeros_like(top),)
        return jnp.concatenate(rows + list(pieces), axis=0)

    for d in q_near:
        q_near[d].wait_recv()
    attend(yh)
    back_near = back_to_x_peers(yh)
    if Z >= 4:
        ring = arrived_first(ring, 2)

    for d in q_far:
        q_far[d].wait_recv()
    attend(1 - yh)
    back_far = back_to_x_peers(1 - yh)
    wait(w_line)
    ring_two = second_ring(1)
    to_sibling(z)
    for step in range(3, Z // 2):
        ring = arrived_first(ring, step)

    wait(back_near)
    ymine[...] = merged(yh)
    wait(back_far)
    ysend[...] = merged(1 - yh).astype(BF16)
    back_y = send(ysend, yrecv, partner)

    loaded("own", "row")
    slots = Z * side * CAP
    owner_row = own_ref[...]
    owner_col = as_column(owner_row)
    square = (samples, samples)
    earlier = (owner_col == owner_row) & (iota(square, 0) < iota(square, 1))
    rank = jnp.sum(jnp.where(earlier, 1, 0), axis=0, keepdims=True)
    slot = owner_row * CAP + rank
    hit = iota((slots, samples), 0) == slot
    table_row = jnp.sum(jnp.where(hit, row_ref[...] + 1, 0), axis=1, keepdims=True) - 1
    xs[:, width:] = (table_row == iota((slots, 128), 1)).astype(F32).astype(BF16)
    hit = hit.astype(F32)
    none = jnp.zeros_like(hit)
    spread = jnp.concatenate(
        [jnp.concatenate([hit, none], axis=1), jnp.concatenate([none, hit], axis=1)], axis=0
    ).astype(BF16)

    if Z >= 4:
        arrived_first(ring, Z // 2)
        ring_two = arrived_second(ring_two, 1)
    back_y.wait_recv()
    rows, unused, total = merge([ymine[...], yrecv[...].astype(F32)])
    picked = jnp.concatenate(
        [rows[h] / total[h:h + 1] for h in range(heads_half)], axis=0
    ).astype(BF16)
    placed = dot(spread, picked, NT).astype(BF16)
    xs[:, 0:half_rows] = placed[0:slots]
    xs[:, half_rows:width] = placed[slots:]

    group = side * CAP

    def rows_of(index):
        return pl.ds(pl.multiple_of(index * group, group), group)

    along_z = [
        send(xs.at[rows_of(lax.rem(z + d, Z))], r1.at[z], z_peer(d)) for d in range(1, Z)
    ]
    r1[z] = xs[rows_of(z), :]
    for step in range(2, Z // 2):
        ring_two = arrived_second(ring_two, step)

    count = Z * CAP
    for copy in along_z:
        copy.wait_recv()
    to_row, from_row = iota((slots, slots), 0), iota((slots, slots), 1)
    wanted = ((to_row // CAP) % Z) * group + (to_row // count) * CAP + to_row % CAP
    order = (wanted == from_row).astype(F32).astype(BF16)
    x2[...] = dot(order, r1[...].reshape(slots, width + 128)).astype(BF16)

    def owner_rows_of(index):
        return pl.ds(pl.multiple_of(index * count, count), count)

    along_side = [
        send(x2.at[owner_rows_of(lax.rem(lane + d, side))], r2.at[lane], side_peer(d))
        for d in range(1, side)
    ]
    r2[lane] = x2[owner_rows_of(lane), :]

    if Z < 4:
        arrived_first(ring, 1)
    wait(e_line)
    e_sibling = send(efull.at[core], efull.at[core], sibling)
    arrived_second(ring_two, Z // 2)
    step_rows = 2 * YL * CORES * shard
    steps = dt // step_rows

    def block_of(ref, half, i, columns):
        return ref[half, pl.ds(2 * i, 2), :, :, columns].reshape(
            step_rows, columns.stop - columns.start
        )

    def columns_of(i):
        return pl.ds(pl.multiple_of(i * step_rows, step_rows), step_rows)

    for copy in along_side:
        copy.wait_recv()
    got = r2[...].reshape(slots, width + 128)
    combine = got[:, width:].astype(F32).T[0:own].astype(BF16)
    grad = dot(combine, got[:, 0:width])
    grad_high = grad.astype(BF16)
    grad_low = (grad - grad_high.astype(F32)).astype(BF16)
    grads = jnp.concatenate([grad_high.astype(F32), grad_low.astype(F32)], axis=0).astype(BF16)

    my_table = pl.ds(pl.multiple_of(yh * own, own), own)

    def project(i, carry):
        every = slice(0, half_rows)
        terms = dot(grads[:, 0:half_rows], block_of(efull, 0, i, every), NT)
        terms += dot(grads[:, half_rows:], block_of(efull, 1, i, every), NT)
        cot_sum[:, columns_of(i)] = terms[0:own] + terms[own:]
        return carry

    e_sibling.wait_recv()
    lax.fori_loop(0, steps, project, 0)
    cot[x, my_table, :] = cot_sum[...].astype(BF16)
    cot_y = send(cot.at[x, my_table], cot.at[x, my_table], partner)
    cot_x = [send(cot.at[x, my_table], cot.at[x, my_table], x_peer(d)) for d in range(1, X)]

    wait(pass_on)
    fwd[...] = jnp.zeros_like(fwd)

    def forward(i, carry):
        rows = normed[:, columns_of(i)]
        fwd[:, 0:part] += dot(rows, block_of(wfull, 0, i, slice(0, part)))
        fwd[:, part:] += dot(rows, block_of(wfull, 1, i, slice(0, cut)))
        return carry

    lax.fori_loop(0, steps, forward, 0)

    cot_y.wait_recv()
    other_table = pl.ds(pl.multiple_of((1 - yh) * own, own), own)
    cot_x += [
        send(cot.at[x, other_table], cot.at[x, other_table], x_peer(d)) for d in range(1, X)
    ]
    wait(cot_x)
    loaded("ls")
    layer_scale = ls_ref[...].reshape(1, dt)
    scaled = (cot[...].reshape(rows_all, dt).astype(F32) * layer_scale).astype(BF16)
    normed[...] = scaled
    hid[...] = jnp.zeros_like(hid)

    def hidden(i, carry):
        hid[...] += dot(normed[:, columns_of(i)], block_of(wfull, 1, i, slice(cut, part)))
        return carry

    lax.fori_loop(0, steps, hidden, 0)
    gate, up, hidden_cot = fwd[:, 0:ff], fwd[:, ff:], hid[...]
    sigmoid = jax.nn.sigmoid(gate)
    gu[:, 0:ff] = (hidden_cot * up * sigmoid * (1.0 + gate * (1.0 - sigmoid))).astype(BF16)
    gu[:, ff:] = (hidden_cot * gate * sigmoid).astype(BF16)

    def backward(i, carry):
        terms = dot(gu[:, 0:part], block_of(wfull, 0, i, slice(0, part)), NT)
        terms += dot(gu[:, part:], block_of(wfull, 1, i, slice(0, cut)), NT)
        rs[:, :, columns_of(i)] = terms.astype(BF16).reshape(X, YH * own, step_rows)
        return carry

    lax.fori_loop(0, steps, backward, 0)
    sum_x = [
        send(rs.at[lax.rem(x + d, X)], rs_in.at[d - 1], x_peer(d)) for d in range(1, X)
    ]

    xhat, inverse = standardize(
        st_ref[0, pl.ds(pl.multiple_of(blk * own, own), own), :].astype(F32)
    )
    for copy in sum_x:
        copy.wait_recv()
    partial = rs[x].astype(F32)
    for d in range(X - 1):
        partial += rs_in[d].astype(F32)

    @pl.when(yh == 0)
    def _():
        ry_send[...] = partial[own:].astype(BF16)
        cot_sum[...] = partial[0:own]

    @pl.when(yh == 1)
    def _():
        ry_send[...] = partial[0:own].astype(BF16)
        cot_sum[...] = partial[own:]

    sum_y = send(ry_send, ry_in, partner)
    sum_y.wait_recv()
    grads_in = (cot_sum[...] + ry_in[...].astype(F32)) * gain
    result = cot[x, my_table, :].astype(F32) + inverse * (
        grads_in
        - jnp.mean(grads_in, axis=-1, keepdims=True)
        - xhat * jnp.mean(grads_in * xhat, axis=-1, keepdims=True)
    )
    out_ref[0] = result.astype(BF16)

    for copy in copies:
        copy.wait_send()


def local(
    queries, key_rows, values, slide_lens, sample_pos, owner_ids, owner_rows, embed_proj,
    tile_states, layernorm_gain, layernorm_bias, layer_scale, w_gate, w_up, w_down,
):
    tokens, width = key_rows.shape[1:]
    samples = sample_pos.shape[1]
    rows_all, dt = tile_states.shape[1:]
    shard, ff = w_gate.shape
    own = rows_all // (X * YH)
    both = 2 * samples
    half_all = width // 2 + STATS
    side = CORES * YL
    slots = Z * side * CAP
    part = 3 * ff // 2
    vmem = pltpu.VMEM
    operands = (
        slide_lens, queries, key_rows, values, sample_pos, owner_ids[:, :, 0], owner_rows,
        embed_proj, tile_states, layernorm_gain, layernorm_bias, layer_scale, w_gate, w_up,
        w_down.T,
    )
    scratch = [pltpu.SMEM(slide_lens.shape, jnp.int32)]
    scratch += [vmem(operand.shape, operand.dtype) for operand in operands[1:]]
    scratch += [
        vmem((YH, X * samples, width), BF16),
        vmem((2, tokens, width), BF16),
        vmem((width, tokens), BF16),
        vmem((tokens, X * samples), F32),
        vmem((2, 2, 8, X * samples), F32),
        vmem((YH, X, half_all, both), BF16),
        vmem((YH, X - 1, half_all, both), BF16),
        vmem((half_all, both), BF16),
        vmem((half_all, both), F32),
        vmem((half_all, both), BF16),
        vmem((slots, width + 128), BF16),
        vmem((Z, side * CAP, width + 128), BF16),
        vmem((slots, width + 128), BF16),
        vmem((side, Z * CAP, width + 128), BF16),
        vmem((X, YH * own, dt), BF16),
        vmem((own, dt), F32),
        vmem((X, YH * own, dt), BF16),
        vmem((X - 1, YH * own, dt), BF16),
        vmem((own, dt), BF16),
        vmem((own, dt), BF16),
        vmem((CORES, shard, part + width // 2), BF16),
        vmem((shard, part + width // 2), BF16),
        vmem((2, Z, YL, CORES * shard, part), BF16),
        vmem((2, Z, YL, CORES * shard, width // 2), BF16),
        vmem((rows_all, dt), BF16),
        vmem((rows_all, 2 * ff), F32),
        vmem((rows_all, ff), F32),
        vmem((rows_all, 2 * ff), BF16),
        pltpu.SemaphoreType.DMA((len(operands),)),
        pltpu.SemaphoreType.DMA((160,)),
        pltpu.SemaphoreType.DMA((160,)),
    ]
    return pl.pallas_call(
        kernel,
        out_shape=jax.ShapeDtypeStruct((1, own, dt), BF16),
        in_specs=[pl.BlockSpec(memory_space=pl.ANY)] * len(operands),
        out_specs=pl.BlockSpec(memory_space=pltpu.VMEM),
        scratch_shapes=scratch,
        compiler_params=pltpu.CompilerParams(
            collective_id=0, has_side_effects=True, vmem_limit_bytes=60 * 1024 * 1024
        ),
    )(*operands)


def solution(mesh):
    return jax.shard_map(
        local,
        mesh=mesh,
        in_specs=(
            P("tile", "blk", None),
            P("tile", "blk", None),
            P("tile", "blk", None),
            P("tile"),
            P("tile", "blk"),
            P("tile", "blk", None),
            P("tile", "blk"),
            P("tile", None),
            P("tile", None, None),
            P(),
            P(),
            P(),
            P("tile", "blk"),
            P("tile", "blk"),
            P("blk", "tile"),
        ),
        out_specs=P("tile", "blk", None),
        check_vma=False,
    )
```

```python
import functools
import math

import jax
import jax.numpy as jnp
from jax import lax
from jax.experimental import pallas as pl
from jax.experimental.pallas import tpu as pltpu
from jax.sharding import PartitionSpec as P

X, YH = 4, 2
Z, YL, CORES = 8, 4, 2
HEAD_DIM = 64
CAP = 2
EPS = 1e-06
NEG = -1e30
FLOOR = -1e29
STATS = 16
SENDS, RECEIVES = 102, 154
F32, BF16 = jnp.float32, jnp.bfloat16
MESH = pl.DeviceIdType.MESH

NT = (((1,), (1,)), ((), ()))
NN = (((1,), (0,)), ((), ()))


def dot(a, b, dims=NN):
    return lax.dot_general(a, b, dims, preferred_element_type=F32)


def iota(shape, axis):
    return lax.broadcasted_iota(jnp.int32, shape, axis)


def as_column(row):
    n = row.shape[1]
    same = iota((n, n), 0) == iota((n, n), 1)
    return jnp.sum(jnp.where(same, row, 0), axis=1, keepdims=True)


def split3(value):
    high = value.astype(BF16).astype(F32)
    rest = value - high
    middle = rest.astype(BF16).astype(F32)
    return high, middle, rest - middle


def standardize(rows):
    centered = rows - jnp.mean(rows, axis=-1, keepdims=True)
    inverse = lax.rsqrt(jnp.mean(centered * centered, axis=-1, keepdims=True) + EPS)
    return centered * inverse, inverse


def kernel(
    len_hbm, q_hbm, k_hbm, v_hbm, pos_hbm, own_hbm, row_hbm, e_hbm, st_hbm,
    gain_hbm, bias_hbm, ls_hbm, wg_hbm, wu_hbm, wd_hbm,
    out_ref,
    len_ref, q_ref, k_ref, v_ref, pos_ref, own_ref, row_ref, e_ref, st_ref,
    gain_ref, bias_ref, ls_ref, wg_ref, wu_ref, wd_ref,
    qall, kmask, vt, mask, stat, ret, ret_in, ysend, ymine, yrecv,
    xs, spread, meta, meta_a, meta_b, combine, r1a, r1b, pa, pb, r2a, r2b, sums, cot, cot_sum, rs, rs_in, ry_send, ry_in,
    wpair, wout, wfull, efull, normed, fwd, hid, gu,
    load_sems, send_sems, recv_sems,
):
    blk, tile = lax.axis_index("blk"), lax.axis_index("tile")
    x, yh = blk // YH, blk % YH
    core = tile % CORES
    yl = (tile // CORES) % YL
    z = tile // (CORES * YL)
    lane = tile % (CORES * YL)
    side = CORES * YL

    tokens, width = k_ref.shape[1], k_ref.shape[2]
    samples = pos_ref.shape[1]
    heads_half = width // HEAD_DIM // 2
    half_rows = width // 2
    ff = wg_ref.shape[1]
    own = out_ref.shape[1]
    rows_all = st_ref.shape[1]
    dt = st_ref.shape[2]
    shard = e_ref.shape[0]
    scale = 1.0 / math.sqrt(HEAD_DIM) * math.log2(math.e)
    part = 3 * ff // 2

    def at(new_x=None, new_yh=None, new_z=None, new_yl=None, new_core=None):
        a = x if new_x is None else new_x
        b = yh if new_yh is None else new_yh
        c = z if new_z is None else new_z
        d = yl if new_yl is None else new_yl
        e = core if new_core is None else new_core
        return (a * YH + b, (c * YL + d) * CORES + e)

    def x_peer(d):
        return at(new_x=lax.rem(x + d, X))

    def z_peer(d):
        return at(new_z=lax.rem(z + d + Z, Z))

    def side_peer(d):
        other = lax.rem(lane + d, side)
        return (blk, z * side + other)

    def y_peer(d):
        place = lax.rem(yh * YL + yl + d + YH * YL, YH * YL)
        return at(new_yh=place // YL, new_yl=place % YL)

    partner = at(new_yh=1 - yh)
    sibling = at(new_core=1 - core)

    barrier = pltpu.get_barrier_semaphore()
    targets = [partner]
    targets += [x_peer(d) for d in range(1, X)]
    targets += [z_peer(d) for d in range(1, Z)]
    targets += [side_peer(d) for d in range(1, side)]
    targets += [y_peer(d) for d in (1, -1, 2, -2)]
    for target in targets:
        pl.semaphore_signal(barrier, inc=1, device_id=target, device_id_type=MESH)

    loads = {}
    for index, (name, source, target) in enumerate([
        ("pos", pos_hbm, pos_ref), ("q", q_hbm, q_ref), ("wg", wg_hbm, wg_ref),
        ("wu", wu_hbm, wu_ref), ("wd", wd_hbm, wd_ref), ("e", e_hbm, e_ref),
        ("len", len_hbm, len_ref), ("k", k_hbm, k_ref), ("v", v_hbm, v_ref),
        ("st", st_hbm, st_ref), ("gain", gain_hbm, gain_ref), ("bias", bias_hbm, bias_ref),
        ("own", own_hbm, own_ref), ("row", row_hbm, row_ref), ("ls", ls_hbm, ls_ref),
    ]):
        loads[name] = pltpu.make_async_copy(source, target, load_sems.at[index])
        loads[name].start()

    def loaded(*names):
        for name in names:
            loads.pop(name).wait()

    copies = []
    live, free, free_of = [], [], []

    def retire(until):
        while live and len(copies) - len(live) < until:
            copy, index = live.pop(0)
            copy.wait_send()
            free.append(index)

    def send(src, dst, target):
        index = free.pop() if free else len(free_of)
        if index == len(free_of):
            free_of.append(index)
        copy = pltpu.make_async_remote_copy(
            src_ref=src, dst_ref=dst,
            send_sem=send_sems.at[index], recv_sem=recv_sems.at[len(copies)],
            device_id=target, device_id_type=MESH,
        )
        copy.start()
        copies.append(copy)
        live.append((copy, index))
        return copy

    loaded("pos", "q")
    chosen = (as_column(pos_ref[...]) == iota((samples, tokens), 1)).astype(F32).astype(BF16)
    my_rows = pl.ds(pl.multiple_of(x * samples, samples), samples)
    qall[yh, my_rows, :] = dot(chosen, q_ref[0]).astype(BF16)

    loaded("wg", "wu", "wd", "e")
    cut = ff // 2

    def fill(mine, first):
        if first:
            mine[:, 0:ff] = wg_ref[...]
            mine[:, ff:part] = wu_ref[:, 0:cut]
            mine[:, part:] = e_ref[:, 0:half_rows]
        else:
            mine[:, 0:cut] = wu_ref[:, cut:]
            mine[:, cut:part] = wd_ref[...]
            mine[:, part:] = e_ref[:, half_rows:]

    @pl.when(core == 0)
    def _():
        fill(wpair.at[0], True)
        fill(wout, False)

    @pl.when(core == 1)
    def _():
        fill(wpair.at[1], False)
        fill(wout, True)

    pl.semaphore_wait(barrier, len(targets))

    parts = [slice(0, half_rows), slice(half_rows, width)]
    q_y = []
    for part_of in parts:
        rows = qall.at[yh, my_rows, part_of]
        q_y.append(send(rows, rows, partner))
    w_pair = send(wout, wpair.at[core], sibling)
    q_near = []
    for d in range(1, X):
        q_near.append(send(qall.at[yh, my_rows], qall.at[yh, my_rows], x_peer(d)))

    w_pair.wait_recv()
    whole = jnp.concatenate([wpair[0].astype(F32), wpair[1].astype(F32)], axis=0).astype(BF16)
    wfull[core, z, yl] = whole[:, 0:part]
    efull[core, z, yl] = whole[:, part:]

    turn = 1 - 2 * core

    def step_blocks(step):
        up, down = lax.rem(z - (step - 1) + Z, Z), lax.rem(z + (step - 1), Z)
        if step < Z // 2:
            return [(up, 1), (down, -1)]
        return [(lax.rem(z - turn * (step - 1) + Z, Z), turn)]

    def first_ring(step):
        return [
            send(ref.at[core, block, yl], ref.at[core, block, yl], z_peer(way))
            for block, way in step_blocks(step)
            for ref in (efull, wfull)
        ]

    def second_ring(step, d):
        sent = []
        for block, way in step_blocks(step):
            place = wfull.at[core, block, lax.rem(yl + d, YL)]
            sent.append(send(place, place, z_peer(way)))
        return sent

    e_line = []

    def e_along_y(block, way):
        place = efull.at[core, block, yl]
        for d in (1, -1, 2 * way):
            e_line.append(send(place, place, y_peer(d)))

    def wait(sent):
        for copy in sent:
            copy.wait_recv()

    pass_on = []

    def to_sibling(block):
        pass_on.append(send(wfull.at[core, block], wfull.at[core, block], sibling))

    def arrived_first(sent, step):
        wait(sent)
        following = None
        if step < Z // 2:
            following = first_ring(step + 1)
            e_along_y(lax.rem(z - step + Z, Z), 1)
            e_along_y(lax.rem(z + step, Z), -1)
        else:
            e_along_y(lax.rem(z + step, Z), 1)
        return following

    def arrived_second(sent, step):
        following = {}
        for d in sent:
            wait(sent[d])
            if step < Z // 2:
                following[d] = second_ring(step + 1, d)
        if step < Z // 2:
            to_sibling(lax.rem(z - step + Z, Z))
        to_sibling(lax.rem(z + step, Z))
        return following

    ring = first_ring(1)

    loaded("len", "k", "v")
    positions = blk * tokens + iota((tokens, X * samples), 0)
    mask[...] = jnp.where(positions < len_ref[0], 0.0, NEG).astype(F32)
    vt[...] = v_ref[0].astype(F32).T.astype(BF16)
    keys = k_ref[0]
    even = iota((tokens, width), 1) % 128 < HEAD_DIM
    kmask[0] = jnp.where(even, keys, jnp.zeros_like(keys))
    kmask[1] = jnp.where(even, jnp.zeros_like(keys), keys)
    stat[...] = jnp.zeros_like(stat)

    loaded("st", "gain", "bias")
    xhat, unused = standardize(st_ref[0].astype(F32))
    gain = gain_ref[...].reshape(1, dt)
    normed[...] = (xhat * gain + bias_ref[...].reshape(1, dt)).astype(BF16)

    loaded("own", "row")
    slots = Z * side * CAP
    owner_row = own_ref[...]
    owner_col = as_column(owner_row)
    square = (samples, samples)
    earlier = (owner_col == owner_row) & (iota(square, 0) < iota(square, 1))
    rank = jnp.sum(jnp.where(earlier, 1, 0), axis=0, keepdims=True)
    slot_a = owner_row * CAP + rank
    slot_b = (owner_row % side) * (Z * CAP) + (owner_row // side) * CAP + rank
    for route, slot in enumerate((slot_a, slot_b)):
        hit = iota((slots, samples), 0) == slot
        table_row = jnp.sum(jnp.where(hit, row_ref[...] + 1, 0), axis=1, keepdims=True) - 1
        meta[route] = (table_row == iota((slots, 128), 1)).astype(F32).astype(BF16)
        hit = hit.astype(F32)
        spread[route] = jnp.concatenate([hit, jnp.zeros_like(hit)], axis=1).astype(BF16)
    group, count = side * CAP, Z * CAP

    def rows_at(index, size):
        return pl.ds(pl.multiple_of(index * size, size), size)

    def first_leg(source, along_z, along_side):
        sent = [
            send(source.at[0, rows_at(lax.rem(z + d, Z), group)], along_z.at[z], z_peer(d))
            for d in range(1, Z)
        ], [
            send(
                source.at[1, rows_at(lax.rem(lane + d, side), count)],
                along_side.at[lane], side_peer(d),
            )
            for d in range(1, side)
        ]
        along_z[z] = source[0, rows_at(z, group), :]
        along_side[lane] = source[1, rows_at(lane, count), :]
        return sent

    meta_sent = first_leg(meta, meta_a, meta_b)

    retire(len(q_y))
    w_line = [
        send(
            wfull.at[core, z, yl], wfull.at[core, z, yl],
            at(new_yl=lax.rem(yl + d, YL)),
        )
        for d in range(1, YL)
    ]
    e_along_y(z, 1)
    ring = arrived_first(ring, 1)

    q_far = []
    for part_of, copy in zip(parts, q_y):
        copy.wait_recv()
        rows = qall.at[1 - yh, my_rows, part_of]
        q_far.append([send(rows, rows, x_peer(d)) for d in range(1, X)])
    def pack(first, second):
        both = 2 * samples
        low = iota((first.shape[0], both), 1) < samples
        pieces = []
        for start in range(0, X * samples, both):
            a, b = first[:, start:start + both], second[:, start:start + both]
            pieces.append(jnp.where(low, a, pltpu.roll(b, samples, 1)))
            pieces.append(jnp.where(low, pltpu.roll(a, samples, 1), b))
        return pieces

    pairs = heads_half // 2
    kept_rows = pairs * HEAD_DIM

    def stats_of(top, total):
        return split3(top) + split3(total)[:2]

    def attend(group, half):
        for pair in range(pairs):
            mixed, tops, totals = [], [], []
            for head in (half * heads_half + pair, half * heads_half + pair + pairs):
                features = slice(head // 2 * 128, head // 2 * 128 + 128)
                scores = dot(kmask[head % 2, :, features], qall[group, :, features], NT)
                scores += mask[...]
                top = jnp.maximum(jnp.max(scores, axis=0, keepdims=True), FLOOR)
                weights = jnp.exp2((scores - top) * scale)
                tops.append(top)
                totals.append(jnp.sum(weights, axis=0, keepdims=True))
                mine = slice(head * HEAD_DIM, head * HEAD_DIM + HEAD_DIM)
                mixed.append(dot(vt[mine, :], weights.astype(BF16)))
            rows = slice(pair * HEAD_DIM, pair * HEAD_DIM + HEAD_DIM)
            packed_tops, packed_totals = pack(*tops), pack(*totals)
            for place, piece in enumerate(pack(*mixed)):
                ret[half, group, place, rows, :] = piece.astype(BF16)
                rows_in = stats_of(packed_tops[place], packed_totals[place])
                for kind, row in enumerate(rows_in):
                    at_row = kind * pairs + pair
                    stat[place, at_row:at_row + 1, :] = row
        for place in range(X):
            ret[half, group, place, kept_rows:, :] = stat[place].astype(BF16)

    def back_to_x_peers(group, half):
        sent = []
        for d in range(1, X):
            place = lax.rem(x + d, X)
            sent.append(
                send(ret.at[half, group, place], ret_in.at[half, group, d - 1], x_peer(d))
            )
        return sent

    def merge(terms):
        stats = [term[kept_rows:] for term in terms]

        def kind(s, index):
            return s[index * pairs:(index + 1) * pairs]

        tops = [kind(s, 0) + kind(s, 1) + kind(s, 2) for s in stats]
        top = functools.reduce(jnp.maximum, tops)
        factors = [jnp.exp2((t - top) * scale) for t in tops]
        total = sum(f * (kind(s, 3) + kind(s, 4)) for f, s in zip(factors, stats))
        rows = []
        for head in range(pairs):
            here = slice(head * HEAD_DIM, head * HEAD_DIM + HEAD_DIM)
            rows.append(sum(f[head:head + 1] * t[here] for f, t in zip(factors, terms)))
        return rows, top, total

    def merged(group, half, target):
        rows, top, total = merge(
            [ret[half, group, x].astype(F32)]
            + [ret_in[half, group, d].astype(F32) for d in range(X - 1)]
        )
        for head in range(pairs):
            target[half, head * HEAD_DIM:(head + 1) * HEAD_DIM, :] = rows[head].astype(
                target.dtype
            )
        for index, pieces in enumerate(stats_of(top, total)):
            stat[0, index * pairs:(index + 1) * pairs, :] = pieces
        target[half, kept_rows:, :] = stat[0].astype(target.dtype)

    wait(q_near)
    for half in range(2):
        attend(yh, half)
    if Z >= 4:
        ring = arrived_first(ring, 2)

    ring_two = {}
    for d in range(1, YL):
        w_line[YL - 1 - d].wait_recv()
        ring_two[d] = second_ring(1, d)
    to_sibling(z)

    back_far = []
    for half in range(2):
        wait(q_far[half])
        attend(1 - yh, half)
        back_far.append(back_to_x_peers(1 - yh, half))
    for step in range(3, Z // 2):
        ring = arrived_first(ring, step)
    begun = len(copies)
    if Z >= 4:
        ring_two = arrived_second(ring_two, 1)

    back_y = []
    for half in range(2):
        wait(back_far[half])
        merged(1 - yh, half, ysend)
        back_y.append(send(ysend.at[half], yrecv.at[half], partner))
    back_near = [back_to_x_peers(yh, half) for half in range(2)]

    if Z >= 4:
        arrived_first(ring, Z // 2)
    if Z >= 6:
        ring_two = arrived_second(ring_two, 2)
    for route, came, others in ((0, meta_a, side), (1, meta_b, Z)):
        wait(meta_sent[route])
        rows = came[...].reshape(slots, 128).astype(F32).T[0:own]
        rows = jnp.concatenate([rows] * others, axis=0)
        shape = (others * own, slots)
        same = iota(shape, 0) // own == (iota(shape, 1) // CAP) % others
        combine[route, 0:others * own, :] = jnp.where(same, rows, 0.0).astype(BF16)

    for half in range(2):
        wait(back_near[half])
        merged(yh, half, ymine)
    retire(begun)
    for half in range(2):
        back_y[half].wait_recv()
        rows, unused, total = merge([ymine[half], yrecv[half].astype(F32)])
        picked = jnp.concatenate([rows[h] / total[h:h + 1] for h in range(pairs)], axis=0)
        picked = jnp.concatenate([picked, pltpu.roll(picked, samples, 1)], axis=0)
        xs[half] = dot(spread[half], picked.astype(BF16), NT).astype(BF16)
    leg_one = first_leg(xs, r1a, r1b)
    for step in range(3, Z // 2):
        ring_two = arrived_second(ring_two, step)

    wait(leg_one[0])
    pa[...] = dot(combine[0, 0:side * own], r1a[...].reshape(slots, half_rows)).astype(BF16)
    leg_two = [
        send(pa.at[rows_at(lax.rem(lane + d, side), own)], r2a.at[lane], side_peer(d))
        for d in range(1, side)
    ]
    r2a[lane] = pa[rows_at(lane, own), :]
    wait(leg_one[1])
    pb[...] = dot(combine[1, 0:Z * own], r1b[...].reshape(slots, half_rows)).astype(BF16)
    leg_two += [
        send(pb.at[rows_at(lax.rem(z + d, Z), own)], r2b.at[z], z_peer(d))
        for d in range(1, Z)
    ]
    r2b[z] = pb[rows_at(z, own), :]
    if Z < 4:
        arrived_first(ring, 1)
    wait(e_line)
    e_sibling = send(efull.at[core], efull.at[core], sibling)
    arrived_second(ring_two, Z // 2)
    step_rows = 2 * YL * CORES * shard
    steps = dt // step_rows

    def block_of(ref, half, i, columns):
        return ref[half, pl.ds(2 * i, 2), :, :, columns].reshape(
            step_rows, columns.stop - columns.start
        )

    def columns_of(i):
        return pl.ds(pl.multiple_of(i * step_rows, step_rows), step_rows)

    wait(leg_two)
    my_table = pl.ds(pl.multiple_of(yh * own, own), own)
    sums[x, my_table, 0:half_rows] = jnp.sum(r2a[...].astype(F32), axis=0).astype(BF16)
    sums[x, my_table, half_rows:] = jnp.sum(r2b[...].astype(F32), axis=0).astype(BF16)
    begun = len(copies)
    sums_y = send(sums.at[x, my_table], sums.at[x, my_table], partner)
    sums_x = [
        send(sums.at[x, my_table], sums.at[x, my_table], x_peer(d)) for d in range(1, X)
    ]

    wait(pass_on)
    fwd[...] = jnp.zeros_like(fwd)

    def forward(i, carry):
        rows = normed[:, columns_of(i)]
        fwd[:, 0:part] += dot(rows, block_of(wfull, 0, i, slice(0, part)))
        fwd[:, part:] += dot(rows, block_of(wfull, 1, i, slice(0, cut)))
        return carry

    lax.fori_loop(0, steps, forward, 0)

    retire(begun)
    sums_y.wait_recv()
    other_table = pl.ds(pl.multiple_of((1 - yh) * own, own), own)
    sums_x += [
        send(sums.at[x, other_table], sums.at[x, other_table], x_peer(d)) for d in range(1, X)
    ]
    e_sibling.wait_recv()
    wait(sums_x)

    def project(i, carry):
        grads, every = sums[...].reshape(rows_all, width), slice(0, half_rows)
        terms = dot(grads[:, 0:half_rows], block_of(efull, 0, i, every), NT)
        terms += dot(grads[:, half_rows:], block_of(efull, 1, i, every), NT)
        cot[:, :, columns_of(i)] = terms.astype(BF16).reshape(X, YH * own, step_rows)
        return carry

    lax.fori_loop(0, steps, project, 0)

    loaded("ls")
    layer_scale = ls_ref[...].reshape(1, dt)
    scaled = (cot[...].reshape(rows_all, dt).astype(F32) * layer_scale).astype(BF16)
    normed[...] = scaled
    hid[...] = jnp.zeros_like(hid)

    def hidden(i, carry):
        hid[...] += dot(normed[:, columns_of(i)], block_of(wfull, 1, i, slice(cut, part)))
        return carry

    lax.fori_loop(0, steps, hidden, 0)
    gate, up, hidden_cot = fwd[:, 0:ff], fwd[:, ff:], hid[...]
    sigmoid = jax.nn.sigmoid(gate)
    gu[:, 0:ff] = (hidden_cot * up * sigmoid * (1.0 + gate * (1.0 - sigmoid))).astype(BF16)
    gu[:, ff:] = (hidden_cot * gate * sigmoid).astype(BF16)

    def backward(i, carry):
        terms = dot(gu[:, 0:part], block_of(wfull, 0, i, slice(0, part)), NT)
        terms += dot(gu[:, part:], block_of(wfull, 1, i, slice(0, cut)), NT)
        rs[:, :, columns_of(i)] = terms.astype(BF16).reshape(X, YH * own, step_rows)
        return carry

    sum_x, sum_y, portions = [], [], 2
    chunks = [slice(c * dt // portions, (c + 1) * dt // portions) for c in range(portions)]
    for c, chunk in enumerate(chunks):
        lax.fori_loop(c * steps // portions, (c + 1) * steps // portions, backward, 0)
        sum_x.append([
            send(
                rs.at[lax.rem(x + d, X), :, chunk], rs_in.at[d - 1, :, chunk], x_peer(d)
            )
            for d in range(1, X)
        ])
    xhat, inverse = standardize(
        st_ref[0, pl.ds(pl.multiple_of(blk * own, own), own), :].astype(F32)
    )
    for c, chunk in enumerate(chunks):
        wait(sum_x[c])
        partial = rs[x, :, chunk].astype(F32)
        for d in range(X - 1):
            partial += rs_in[d, :, chunk].astype(F32)
        cot_sum[:, chunk] = partial
        ry_send[:, chunk] = cot_sum[other_table, chunk].astype(BF16)
        sum_y.append(send(ry_send.at[:, chunk], ry_in.at[:, chunk], partner))
    base = cot[x, my_table, :].astype(F32)
    retire(len(copies) - len(sum_y))
    wait(sum_y)
    grads_in = (cot_sum[my_table, :] + ry_in[...].astype(F32)) * gain
    result = base + inverse * (
        grads_in
        - jnp.mean(grads_in, axis=-1, keepdims=True)
        - xhat * jnp.mean(grads_in * xhat, axis=-1, keepdims=True)
    )
    out_ref[0] = result.astype(BF16)

    retire(len(copies))


def local(
    queries, key_rows, values, slide_lens, sample_pos, owner_ids, owner_rows, embed_proj,
    tile_states, layernorm_gain, layernorm_bias, layer_scale, w_gate, w_up, w_down,
):
    tokens, width = key_rows.shape[1:]
    samples = sample_pos.shape[1]
    rows_all, dt = tile_states.shape[1:]
    shard, ff = w_gate.shape
    own = rows_all // (X * YH)
    both = 2 * samples
    half = width // 2
    part_rows = half // 2 + STATS
    side = CORES * YL
    slots = Z * side * CAP
    part = 3 * ff // 2
    vmem = pltpu.VMEM
    operands = (
        slide_lens, queries, key_rows, values, sample_pos, owner_ids[:, :, 0], owner_rows,
        embed_proj, tile_states, layernorm_gain, layernorm_bias, layer_scale, w_gate, w_up,
        w_down.T,
    )
    scratch = [pltpu.SMEM(slide_lens.shape, jnp.int32)]
    scratch += [vmem(operand.shape, operand.dtype) for operand in operands[1:]]
    scratch += [
        vmem((YH, X * samples, width), BF16),
        vmem((2, tokens, width), BF16),
        vmem((width, tokens), BF16),
        vmem((tokens, X * samples), F32),
        vmem((X, STATS, both), F32),
        vmem((2, YH, X, part_rows, both), BF16),
        vmem((2, YH, X - 1, part_rows, both), BF16),
        vmem((2, part_rows, both), BF16),
        vmem((2, part_rows, both), F32),
        vmem((2, part_rows, both), BF16),
        vmem((2, slots, half), BF16),
        vmem((2, slots, both), BF16),
        vmem((2, slots, 128), BF16),
        vmem((Z, side * CAP, 128), BF16),
        vmem((side, Z * CAP, 128), BF16),
        vmem((2, side * own, slots), BF16),
        vmem((Z, side * CAP, half), BF16),
        vmem((side, Z * CAP, half), BF16),
        vmem((side * own, half), BF16),
        vmem((Z * own, half), BF16),
        vmem((side, own, half), BF16),
        vmem((Z, own, half), BF16),
        vmem((X, YH * own, width), BF16),
        vmem((X, YH * own, dt), BF16),
        vmem((YH * own, dt), F32),
        vmem((X, YH * own, dt), BF16),
        vmem((X - 1, YH * own, dt), BF16),
        vmem((own, dt), BF16),
        vmem((own, dt), BF16),
        vmem((CORES, shard, part + width // 2), BF16),
        vmem((shard, part + width // 2), BF16),
        vmem((2, Z, YL, CORES * shard, part), BF16),
        vmem((2, Z, YL, CORES * shard, width // 2), BF16),
        vmem((rows_all, dt), BF16),
        vmem((rows_all, 2 * ff), F32),
        vmem((rows_all, ff), F32),
        vmem((rows_all, 2 * ff), BF16),
        pltpu.SemaphoreType.DMA((len(operands),)),
        pltpu.SemaphoreType.DMA((SENDS,)),
        pltpu.SemaphoreType.DMA((RECEIVES,)),
    ]
    return pl.pallas_call(
        kernel,
        out_shape=jax.ShapeDtypeStruct((1, own, dt), BF16),
        in_specs=[pl.BlockSpec(memory_space=pl.ANY)] * len(operands),
        out_specs=pl.BlockSpec(memory_space=pltpu.VMEM),
        scratch_shapes=scratch,
        compiler_params=pltpu.CompilerParams(
            collective_id=0, has_side_effects=True, vmem_limit_bytes=60 * 1024 * 1024
        ),
    )(*operands)


def solution(mesh):
    return jax.shard_map(
        local,
        mesh=mesh,
        in_specs=(
            P("tile", "blk", None),
            P("tile", "blk", None),
            P("tile", "blk", None),
            P("tile"),
            P("tile", "blk"),
            P("tile", "blk", None),
            P("tile", "blk"),
            P("tile", None),
            P("tile", None, None),
            P(),
            P(),
            P(),
            P("tile", "blk"),
            P("tile", "blk"),
            P("blk", "tile"),
        ),
        out_specs=P("tile", "blk", None),
        check_vma=False,
    )
```

```python
import functools
import math

import jax
import jax.numpy as jnp
from jax import lax
from jax.experimental import pallas as pl
from jax.experimental.pallas import tpu as pltpu
from jax.sharding import PartitionSpec as P

X, YH = 4, 2
Z, YL, CORES = 8, 4, 2
HEAD_DIM = 64
CAP = 2
EPS = 1e-06
NEG = -1e30
FLOOR = -1e29
STATS = 16
SENDS, RECEIVES = 34, 51
F32, BF16 = jnp.float32, jnp.bfloat16
MESH = pl.DeviceIdType.MESH

NT = (((1,), (1,)), ((), ()))
NN = (((1,), (0,)), ((), ()))


def dot(a, b, dims=NN):
    return lax.dot_general(a, b, dims, preferred_element_type=F32)


def iota(shape, axis):
    return lax.broadcasted_iota(jnp.int32, shape, axis)


def as_column(row):
    n = row.shape[1]
    same = iota((n, n), 0) == iota((n, n), 1)
    return jnp.sum(jnp.where(same, row, 0), axis=1, keepdims=True)


def split3(value):
    high = value.astype(BF16).astype(F32)
    rest = value - high
    middle = rest.astype(BF16).astype(F32)
    return high, middle, rest - middle


def standardize(rows):
    centered = rows - jnp.mean(rows, axis=-1, keepdims=True)
    inverse = lax.rsqrt(jnp.mean(centered * centered, axis=-1, keepdims=True) + EPS)
    return centered * inverse, inverse


def kernel(
    len_hbm, q_hbm, k_hbm, v_hbm, pos_hbm, own_hbm, row_hbm, e_hbm, st_hbm,
    gain_hbm, bias_hbm, ls_hbm, wg_hbm, wu_hbm, wd_hbm,
    out_ref,
    len_ref, q_ref, k_ref, v_ref, pos_ref, own_ref, row_ref, e_ref, st_ref,
    gain_ref, bias_ref, ls_ref, wg_ref, wu_ref, wd_ref,
    qall, kmask, vt, mask, stat, ret, ret_in, ysend, ymine, yrecv,
    xs, spread, meta, meta_a, meta_b, combine, r1a, r1b, pa, pb, r2a, r2b, sums, cot, cot_sum, rs, rs_in, ry_send, ry_in,
    wpair, wout, wfull, efull, normed, fwd, hid, gu,
    load_sems, send_sems, recv_sems,
):
    blk, tile = lax.axis_index("blk"), lax.axis_index("tile")
    x, yh = blk // YH, blk % YH
    core = tile % CORES
    yl = (tile // CORES) % YL
    z = tile // (CORES * YL)
    lane = tile % (CORES * YL)
    side = CORES * YL

    tokens, width = k_ref.shape[1], k_ref.shape[2]
    samples = pos_ref.shape[1]
    heads_half = width // HEAD_DIM // 2
    half_rows = width // 2
    ff = wg_ref.shape[1]
    own = out_ref.shape[1]
    rows_all = st_ref.shape[1]
    dt = st_ref.shape[2]
    shard = e_ref.shape[0]
    scale = 1.0 / math.sqrt(HEAD_DIM) * math.log2(math.e)
    part = 3 * ff // 2

    def at(new_x=None, new_yh=None, new_z=None, new_yl=None, new_core=None):
        a = x if new_x is None else new_x
        b = yh if new_yh is None else new_yh
        c = z if new_z is None else new_z
        d = yl if new_yl is None else new_yl
        e = core if new_core is None else new_core
        return (a * YH + b, (c * YL + d) * CORES + e)

    def x_peer(d):
        return at(new_x=lax.rem(x + d, X))

    def z_peer(d):
        return at(new_z=lax.rem(z + d + Z, Z))

    def side_peer(d):
        other = lax.rem(lane + d, side)
        return (blk, z * side + other)

    def y_peer(d):
        place = lax.rem(yh * YL + yl + d + YH * YL, YH * YL)
        return at(new_yh=place // YL, new_yl=place % YL)

    partner = at(new_yh=1 - yh)
    sibling = at(new_core=1 - core)

    barrier = pltpu.get_barrier_semaphore()
    targets = [partner]
    targets += [x_peer(d) for d in range(1, X)]
    targets += [z_peer(d) for d in range(1, Z)]
    targets += [side_peer(d) for d in range(1, side)]
    targets += [y_peer(d) for d in (1, -1, 2, -2)]
    for target in targets:
        pl.semaphore_signal(barrier, inc=1, device_id=target, device_id_type=MESH)

    loads = {}
    for index, (name, source, target) in enumerate([
        ("pos", pos_hbm, pos_ref), ("q", q_hbm, q_ref), ("wg", wg_hbm, wg_ref),
        ("wu", wu_hbm, wu_ref), ("wd", wd_hbm, wd_ref), ("e", e_hbm, e_ref),
        ("len", len_hbm, len_ref), ("k", k_hbm, k_ref), ("v", v_hbm, v_ref),
        ("st", st_hbm, st_ref), ("gain", gain_hbm, gain_ref), ("bias", bias_hbm, bias_ref),
        ("own", own_hbm, own_ref), ("row", row_hbm, row_ref), ("ls", ls_hbm, ls_ref),
    ]):
        loads[name] = pltpu.make_async_copy(source, target, load_sems.at[index])
        loads[name].start()

    def loaded(*names):
        for name in names:
            loads.pop(name).wait()

    copies = []
    live, free, free_of, numbers = [], [], [], []

    def retire(until):
        while live and len(copies) - len(live) < until:
            copy, index = live.pop(0)
            copy.wait_send()
            free.append(index)

    def together(ref, open_end=False):
        return {"ref": ref, "open": open_end}

    def remote(src, dst, target, index, number):
        return pltpu.make_async_remote_copy(
            src_ref=src, dst_ref=dst,
            send_sem=send_sems.at[index], recv_sem=recv_sems.at[number],
            device_id=target, device_id_type=MESH,
        )

    def send(src, dst, target, among=None):
        if among is not None and "copy" in among:
            remote(src, dst, target, among["index"], among["number"]).start()
            return among["copy"]
        index = free.pop() if free else len(free_of)
        if index == len(free_of):
            free_of.append(index)
        number = len(numbers)
        numbers.append(number)
        copy = remote(src, dst, target, index, number)
        copy.start()
        if among is not None:
            ref = among["ref"]
            copy = remote(ref, ref, target, index, number)
            among.update(copy=copy, index=index, number=number)
        if among is None or not among["open"]:
            copies.append(copy)
            live.append((copy, index))
        return copy

    def take(among):
        among["copy"].wait_recv()
        if among["open"]:
            copies.append(among["copy"])
            live.append((among["copy"], among["index"]))

    loaded("pos", "q")
    chosen = (as_column(pos_ref[...]) == iota((samples, tokens), 1)).astype(F32).astype(BF16)
    my_rows = pl.ds(pl.multiple_of(x * samples, samples), samples)
    qall[yh, my_rows, :] = dot(chosen, q_ref[0]).astype(BF16)

    loaded("wg", "wu", "wd", "e")
    cut = ff // 2

    def fill(mine, first):
        if first:
            mine[:, 0:ff] = wg_ref[...]
            mine[:, ff:part] = wu_ref[:, 0:cut]
            mine[:, part:] = e_ref[:, 0:half_rows]
        else:
            mine[:, 0:cut] = wu_ref[:, cut:]
            mine[:, cut:part] = wd_ref[...]
            mine[:, part:] = e_ref[:, half_rows:]

    @pl.when(core == 0)
    def _():
        fill(wpair.at[0], True)
        fill(wout, False)

    @pl.when(core == 1)
    def _():
        fill(wpair.at[1], False)
        fill(wout, True)

    pl.semaphore_wait(barrier, len(targets))

    parts = [slice(0, half_rows), slice(half_rows, width)]
    q_y = []
    for part_of in parts:
        rows = qall.at[yh, my_rows, part_of]
        q_y.append(send(rows, rows, partner))
    w_pair = send(wout, wpair.at[core], sibling)
    three = pl.ds(0, (X - 1) * samples)
    q_near = together(qall.at[0, three])
    for d in range(1, X):
        send(qall.at[yh, my_rows], qall.at[yh, my_rows], x_peer(d), q_near)

    w_pair.wait_recv()
    whole = jnp.concatenate([wpair[0].astype(F32), wpair[1].astype(F32)], axis=0).astype(BF16)
    wfull[core, z, yl] = whole[:, 0:part]
    efull[core, z, yl] = whole[:, part:]

    turn = 1 - 2 * core

    def step_blocks(step):
        up, down = lax.rem(z - (step - 1) + Z, Z), lax.rem(z + (step - 1), Z)
        if step < Z // 2:
            return [(up, 1), (down, -1)]
        return [(lax.rem(z - turn * (step - 1) + Z, Z), turn)]

    def first_ring(step):
        groups = []
        for ref in (efull, wfull):
            blocks = step_blocks(step)
            groups.append(together(ref.at[core, 0:len(blocks), 0]))
            for block, way in blocks:
                place = ref.at[core, block, yl]
                send(place, place, z_peer(way), groups[-1])
        return groups

    def second_ring(step, d):
        blocks = step_blocks(step)
        group = together(wfull.at[core, 0:len(blocks), 0])
        for block, way in blocks:
            place = wfull.at[core, block, lax.rem(yl + d, YL)]
            send(place, place, z_peer(way), group)
        return group

    e_line = together(efull.at[core, :, 0:YL - 1], True)

    def e_along_y(block, way):
        place = efull.at[core, block, yl]
        for d in (1, -1, 2 * way):
            send(place, place, y_peer(d), e_line)

    def wait(sent):
        for copy in sent:
            copy.wait_recv()

    pass_on = together(wfull.at[core], True)

    def to_sibling(block):
        send(wfull.at[core, block], wfull.at[core, block], sibling, pass_on)

    def arrived_first(sent, step):
        for group in sent:
            take(group)
        following = None
        if step < Z // 2:
            following = first_ring(step + 1)
            e_along_y(lax.rem(z - step + Z, Z), 1)
            e_along_y(lax.rem(z + step, Z), -1)
        else:
            e_along_y(lax.rem(z + step, Z), 1)
        return following

    def arrived_second(sent, step):
        following = {}
        for d in sent:
            take(sent[d])
            if step < Z // 2:
                following[d] = second_ring(step + 1, d)
        if step < Z // 2:
            to_sibling(lax.rem(z - step + Z, Z))
        to_sibling(lax.rem(z + step, Z))
        return following

    ring = first_ring(1)

    loaded("len", "k", "v")
    positions = blk * tokens + iota((tokens, X * samples), 0)
    mask[...] = jnp.where(positions < len_ref[0], 0.0, NEG).astype(F32)
    vt[...] = v_ref[0].astype(F32).T.astype(BF16)
    keys = k_ref[0]
    even = iota((tokens, width), 1) % 128 < HEAD_DIM
    kmask[0] = jnp.where(even, keys, jnp.zeros_like(keys))
    kmask[1] = jnp.where(even, jnp.zeros_like(keys), keys)
    stat[...] = jnp.zeros_like(stat)

    loaded("st", "gain", "bias")
    xhat, unused = standardize(st_ref[0].astype(F32))
    gain = gain_ref[...].reshape(1, dt)
    normed[...] = (xhat * gain + bias_ref[...].reshape(1, dt)).astype(BF16)

    loaded("own", "row")
    slots = Z * side * CAP
    owner_row = own_ref[...]
    owner_col = as_column(owner_row)
    square = (samples, samples)
    earlier = (owner_col == owner_row) & (iota(square, 0) < iota(square, 1))
    rank = jnp.sum(jnp.where(earlier, 1, 0), axis=0, keepdims=True)
    slot_a = owner_row * CAP + rank
    slot_b = (owner_row % side) * (Z * CAP) + (owner_row // side) * CAP + rank
    for route, slot in enumerate((slot_a, slot_b)):
        hit = iota((slots, samples), 0) == slot
        table_row = jnp.sum(jnp.where(hit, row_ref[...] + 1, 0), axis=1, keepdims=True) - 1
        meta[route] = (table_row == iota((slots, 128), 1)).astype(F32).astype(BF16)
        hit = hit.astype(F32)
        spread[route] = jnp.concatenate([hit, jnp.zeros_like(hit)], axis=1).astype(BF16)
    group, count = side * CAP, Z * CAP

    def rows_at(index, size):
        return pl.ds(pl.multiple_of(index * size, size), size)

    def first_leg(source, along_z, along_side):
        sent = together(along_z.at[0:Z - 1]), together(along_side.at[0:side - 1])
        for d in range(1, Z):
            rows = rows_at(lax.rem(z + d, Z), group)
            send(source.at[0, rows], along_z.at[z], z_peer(d), sent[0])
        for d in range(1, side):
            rows = rows_at(lax.rem(lane + d, side), count)
            send(source.at[1, rows], along_side.at[lane], side_peer(d), sent[1])
        along_z[z] = source[0, rows_at(z, group), :]
        along_side[lane] = source[1, rows_at(lane, count), :]
        return sent

    meta_sent = first_leg(meta, meta_a, meta_b)

    retire(len(q_y))
    w_line = [
        send(
            wfull.at[core, z, yl], wfull.at[core, z, yl],
            at(new_yl=lax.rem(yl + d, YL)),
        )
        for d in range(1, YL)
    ]
    e_along_y(z, 1)
    ring = arrived_first(ring, 1)

    q_far = []
    for part_of, copy in zip(parts, q_y):
        copy.wait_recv()
        rows = qall.at[1 - yh, my_rows, part_of]
        q_far.append(together(qall.at[0, three, part_of]))
        for d in range(1, X):
            send(rows, rows, x_peer(d), q_far[-1])
    def pack(first, second):
        both = 2 * samples
        low = iota((first.shape[0], both), 1) < samples
        pieces = []
        for start in range(0, X * samples, both):
            a, b = first[:, start:start + both], second[:, start:start + both]
            pieces.append(jnp.where(low, a, pltpu.roll(b, samples, 1)))
            pieces.append(jnp.where(low, pltpu.roll(a, samples, 1), b))
        return pieces

    pairs = heads_half // 2
    kept_rows = pairs * HEAD_DIM

    def stats_of(top, total):
        return split3(top) + split3(total)[:2]

    def attend(group, half):
        for pair in range(pairs):
            mixed, tops, totals = [], [], []
            for head in (half * heads_half + pair, half * heads_half + pair + pairs):
                features = slice(head // 2 * 128, head // 2 * 128 + 128)
                scores = dot(kmask[head % 2, :, features], qall[group, :, features], NT)
                scores += mask[...]
                top = jnp.maximum(jnp.max(scores, axis=0, keepdims=True), FLOOR)
                weights = jnp.exp2((scores - top) * scale)
                tops.append(top)
                totals.append(jnp.sum(weights, axis=0, keepdims=True))
                mine = slice(head * HEAD_DIM, head * HEAD_DIM + HEAD_DIM)
                mixed.append(dot(vt[mine, :], weights.astype(BF16)))
            rows = slice(pair * HEAD_DIM, pair * HEAD_DIM + HEAD_DIM)
            packed_tops, packed_totals = pack(*tops), pack(*totals)
            for place, piece in enumerate(pack(*mixed)):
                ret[half, group, place, rows, :] = piece.astype(BF16)
                rows_in = stats_of(packed_tops[place], packed_totals[place])
                for kind, row in enumerate(rows_in):
                    at_row = kind * pairs + pair
                    stat[place, at_row:at_row + 1, :] = row
        for place in range(X):
            ret[half, group, place, kept_rows:, :] = stat[place].astype(BF16)

    def back_to_x_peers(group, half):
        sent = together(ret_in.at[half, group])
        for d in range(1, X):
            place = lax.rem(x + d, X)
            send(ret.at[half, group, place], ret_in.at[half, group, d - 1], x_peer(d), sent)
        return sent

    def merge(terms):
        stats = [term[kept_rows:] for term in terms]

        def kind(s, index):
            return s[index * pairs:(index + 1) * pairs]

        tops = [kind(s, 0) + kind(s, 1) + kind(s, 2) for s in stats]
        top = functools.reduce(jnp.maximum, tops)
        factors = [jnp.exp2((t - top) * scale) for t in tops]
        total = sum(f * (kind(s, 3) + kind(s, 4)) for f, s in zip(factors, stats))
        rows = []
        for head in range(pairs):
            here = slice(head * HEAD_DIM, head * HEAD_DIM + HEAD_DIM)
            rows.append(sum(f[head:head + 1] * t[here] for f, t in zip(factors, terms)))
        return rows, top, total

    def merged(group, half, target):
        rows, top, total = merge(
            [ret[half, group, x].astype(F32)]
            + [ret_in[half, group, d].astype(F32) for d in range(X - 1)]
        )
        for head in range(pairs):
            target[half, head * HEAD_DIM:(head + 1) * HEAD_DIM, :] = rows[head].astype(
                target.dtype
            )
        for index, pieces in enumerate(stats_of(top, total)):
            stat[0, index * pairs:(index + 1) * pairs, :] = pieces
        target[half, kept_rows:, :] = stat[0].astype(target.dtype)

    take(q_near)
    for half in range(2):
        attend(yh, half)
    if Z >= 4:
        ring = arrived_first(ring, 2)

    ring_two = {}
    for d in range(1, YL):
        w_line[YL - 1 - d].wait_recv()
        ring_two[d] = second_ring(1, d)
    to_sibling(z)

    back_far = []
    for half in range(2):
        take(q_far[half])
        attend(1 - yh, half)
        back_far.append(back_to_x_peers(1 - yh, half))
    for step in range(3, Z // 2):
        ring = arrived_first(ring, step)
    begun = len(copies)
    if Z >= 4:
        ring_two = arrived_second(ring_two, 1)

    back_y = []
    for half in range(2):
        take(back_far[half])
        merged(1 - yh, half, ysend)
        back_y.append(send(ysend.at[half], yrecv.at[half], partner))
    back_near = [back_to_x_peers(yh, half) for half in range(2)]

    if Z >= 4:
        arrived_first(ring, Z // 2)
    if Z >= 6:
        ring_two = arrived_second(ring_two, 2)
    for route, came, others in ((0, meta_a, side), (1, meta_b, Z)):
        take(meta_sent[route])
        rows = came[...].reshape(slots, 128).astype(F32).T[0:own]
        rows = jnp.concatenate([rows] * others, axis=0)
        shape = (others * own, slots)
        same = iota(shape, 0) // own == (iota(shape, 1) // CAP) % others
        combine[route, 0:others * own, :] = jnp.where(same, rows, 0.0).astype(BF16)

    for half in range(2):
        take(back_near[half])
        merged(yh, half, ymine)
    retire(begun)
    for half in range(2):
        back_y[half].wait_recv()
        rows, unused, total = merge([ymine[half], yrecv[half].astype(F32)])
        picked = jnp.concatenate([rows[h] / total[h:h + 1] for h in range(pairs)], axis=0)
        picked = jnp.concatenate([picked, pltpu.roll(picked, samples, 1)], axis=0)
        xs[half] = dot(spread[half], picked.astype(BF16), NT).astype(BF16)
    leg_one = first_leg(xs, r1a, r1b)
    for step in range(3, Z // 2):
        ring_two = arrived_second(ring_two, step)

    take(leg_one[0])
    pa[...] = dot(combine[0, 0:side * own], r1a[...].reshape(slots, half_rows)).astype(BF16)
    leg_two = [together(r2a.at[0:side - 1]), together(r2b.at[0:Z - 1])]
    for d in range(1, side):
        rows = rows_at(lax.rem(lane + d, side), own)
        send(pa.at[rows], r2a.at[lane], side_peer(d), leg_two[0])
    r2a[lane] = pa[rows_at(lane, own), :]
    take(leg_one[1])
    pb[...] = dot(combine[1, 0:Z * own], r1b[...].reshape(slots, half_rows)).astype(BF16)
    for d in range(1, Z):
        send(pb.at[rows_at(lax.rem(z + d, Z), own)], r2b.at[z], z_peer(d), leg_two[1])
    r2b[z] = pb[rows_at(z, own), :]
    if Z < 4:
        arrived_first(ring, 1)
    take(e_line)
    e_sibling = send(efull.at[core], efull.at[core], sibling)
    arrived_second(ring_two, Z // 2)
    step_rows = 2 * YL * CORES * shard
    steps = dt // step_rows

    def block_of(ref, half, i, columns):
        return ref[half, pl.ds(2 * i, 2), :, :, columns].reshape(
            step_rows, columns.stop - columns.start
        )

    def columns_of(i):
        return pl.ds(pl.multiple_of(i * step_rows, step_rows), step_rows)

    for group_of in leg_two:
        take(group_of)
    my_table = pl.ds(pl.multiple_of(yh * own, own), own)
    sums[x, my_table, 0:half_rows] = jnp.sum(r2a[...].astype(F32), axis=0).astype(BF16)
    sums[x, my_table, half_rows:] = jnp.sum(r2b[...].astype(F32), axis=0).astype(BF16)
    begun = len(copies)
    sums_y = send(sums.at[x, my_table], sums.at[x, my_table], partner)
    sums_x = [together(sums.at[0:X - 1, 0:own]) for unused in range(2)]
    for d in range(1, X):
        send(sums.at[x, my_table], sums.at[x, my_table], x_peer(d), sums_x[0])

    take(pass_on)
    fwd[...] = jnp.zeros_like(fwd)

    def forward(i, carry):
        rows = normed[:, columns_of(i)]
        fwd[:, 0:part] += dot(rows, block_of(wfull, 0, i, slice(0, part)))
        fwd[:, part:] += dot(rows, block_of(wfull, 1, i, slice(0, cut)))
        return carry

    lax.fori_loop(0, steps, forward, 0)

    retire(begun)
    sums_y.wait_recv()
    other_table = pl.ds(pl.multiple_of((1 - yh) * own, own), own)
    for d in range(1, X):
        send(sums.at[x, other_table], sums.at[x, other_table], x_peer(d), sums_x[1])
    e_sibling.wait_recv()
    for group_of in sums_x:
        take(group_of)

    def project(i, carry):
        grads, every = sums[...].reshape(rows_all, width), slice(0, half_rows)
        terms = dot(grads[:, 0:half_rows], block_of(efull, 0, i, every), NT)
        terms += dot(grads[:, half_rows:], block_of(efull, 1, i, every), NT)
        cot[:, :, columns_of(i)] = terms.astype(BF16).reshape(X, YH * own, step_rows)
        return carry

    lax.fori_loop(0, steps, project, 0)

    loaded("ls")
    layer_scale = ls_ref[...].reshape(1, dt)
    scaled = (cot[...].reshape(rows_all, dt).astype(F32) * layer_scale).astype(BF16)
    normed[...] = scaled
    hid[...] = jnp.zeros_like(hid)

    def hidden(i, carry):
        hid[...] += dot(normed[:, columns_of(i)], block_of(wfull, 1, i, slice(cut, part)))
        return carry

    lax.fori_loop(0, steps, hidden, 0)
    gate, up, hidden_cot = fwd[:, 0:ff], fwd[:, ff:], hid[...]
    sigmoid = jax.nn.sigmoid(gate)
    gu[:, 0:ff] = (hidden_cot * up * sigmoid * (1.0 + gate * (1.0 - sigmoid))).astype(BF16)
    gu[:, ff:] = (hidden_cot * gate * sigmoid).astype(BF16)

    def backward(i, carry):
        terms = dot(gu[:, 0:part], block_of(wfull, 0, i, slice(0, part)), NT)
        terms += dot(gu[:, part:], block_of(wfull, 1, i, slice(0, cut)), NT)
        rs[:, :, columns_of(i)] = terms.astype(BF16).reshape(X, YH * own, step_rows)
        return carry

    sum_x, sum_y, portions = [], [], 2
    chunks = [slice(c * dt // portions, (c + 1) * dt // portions) for c in range(portions)]
    for c, chunk in enumerate(chunks):
        lax.fori_loop(c * steps // portions, (c + 1) * steps // portions, backward, 0)
        sum_x.append(together(rs_in.at[:, :, chunk]))
        for d in range(1, X):
            other = rs.at[lax.rem(x + d, X), :, chunk]
            send(other, rs_in.at[d - 1, :, chunk], x_peer(d), sum_x[c])
    xhat, inverse = standardize(
        st_ref[0, pl.ds(pl.multiple_of(blk * own, own), own), :].astype(F32)
    )
    for c, chunk in enumerate(chunks):
        take(sum_x[c])
        partial = rs[x, :, chunk].astype(F32)
        for d in range(X - 1):
            partial += rs_in[d, :, chunk].astype(F32)
        cot_sum[:, chunk] = partial
        ry_send[:, chunk] = cot_sum[other_table, chunk].astype(BF16)
        sum_y.append(send(ry_send.at[:, chunk], ry_in.at[:, chunk], partner))
    base = cot[x, my_table, :].astype(F32)
    retire(len(copies) - len(sum_y))
    wait(sum_y)
    grads_in = (cot_sum[my_table, :] + ry_in[...].astype(F32)) * gain
    result = base + inverse * (
        grads_in
        - jnp.mean(grads_in, axis=-1, keepdims=True)
        - xhat * jnp.mean(grads_in * xhat, axis=-1, keepdims=True)
    )
    out_ref[0] = result.astype(BF16)

    retire(len(copies))


def local(
    queries, key_rows, values, slide_lens, sample_pos, owner_ids, owner_rows, embed_proj,
    tile_states, layernorm_gain, layernorm_bias, layer_scale, w_gate, w_up, w_down,
):
    tokens, width = key_rows.shape[1:]
    samples = sample_pos.shape[1]
    rows_all, dt = tile_states.shape[1:]
    shard, ff = w_gate.shape
    own = rows_all // (X * YH)
    both = 2 * samples
    half = width // 2
    part_rows = half // 2 + STATS
    side = CORES * YL
    slots = Z * side * CAP
    part = 3 * ff // 2
    vmem = pltpu.VMEM
    operands = (
        slide_lens, queries, key_rows, values, sample_pos, owner_ids[:, :, 0], owner_rows,
        embed_proj, tile_states, layernorm_gain, layernorm_bias, layer_scale, w_gate, w_up,
        w_down.T,
    )
    scratch = [pltpu.SMEM(slide_lens.shape, jnp.int32)]
    scratch += [vmem(operand.shape, operand.dtype) for operand in operands[1:]]
    scratch += [
        vmem((YH, X * samples, width), BF16),
        vmem((2, tokens, width), BF16),
        vmem((width, tokens), BF16),
        vmem((tokens, X * samples), F32),
        vmem((X, STATS, both), F32),
        vmem((2, YH, X, part_rows, both), BF16),
        vmem((2, YH, X - 1, part_rows, both), BF16),
        vmem((2, part_rows, both), BF16),
        vmem((2, part_rows, both), F32),
        vmem((2, part_rows, both), BF16),
        vmem((2, slots, half), BF16),
        vmem((2, slots, both), BF16),
        vmem((2, slots, 128), BF16),
        vmem((Z, side * CAP, 128), BF16),
        vmem((side, Z * CAP, 128), BF16),
        vmem((2, side * own, slots), BF16),
        vmem((Z, side * CAP, half), BF16),
        vmem((side, Z * CAP, half), BF16),
        vmem((side * own, half), BF16),
        vmem((Z * own, half), BF16),
        vmem((side, own, half), BF16),
        vmem((Z, own, half), BF16),
        vmem((X, YH * own, width), BF16),
        vmem((X, YH * own, dt), BF16),
        vmem((YH * own, dt), F32),
        vmem((X, YH * own, dt), BF16),
        vmem((X - 1, YH * own, dt), BF16),
        vmem((own, dt), BF16),
        vmem((own, dt), BF16),
        vmem((CORES, shard, part + width // 2), BF16),
        vmem((shard, part + width // 2), BF16),
        vmem((2, Z, YL, CORES * shard, part), BF16),
        vmem((2, Z, YL, CORES * shard, width // 2), BF16),
        vmem((rows_all, dt), BF16),
        vmem((rows_all, 2 * ff), F32),
        vmem((rows_all, ff), F32),
        vmem((rows_all, 2 * ff), BF16),
        pltpu.SemaphoreType.DMA((len(operands),)),
        pltpu.SemaphoreType.DMA((SENDS,)),
        pltpu.SemaphoreType.DMA((RECEIVES,)),
    ]
    return pl.pallas_call(
        kernel,
        out_shape=jax.ShapeDtypeStruct((1, own, dt), BF16),
        in_specs=[pl.BlockSpec(memory_space=pl.ANY)] * len(operands),
        out_specs=pl.BlockSpec(memory_space=pltpu.VMEM),
        scratch_shapes=scratch,
        compiler_params=pltpu.CompilerParams(
            collective_id=0, has_side_effects=True, vmem_limit_bytes=60 * 1024 * 1024
        ),
    )(*operands)


def solution(mesh):
    return jax.shard_map(
        local,
        mesh=mesh,
        in_specs=(
            P("tile", "blk", None),
            P("tile", "blk", None),
            P("tile", "blk", None),
            P("tile"),
            P("tile", "blk"),
            P("tile", "blk", None),
            P("tile", "blk"),
            P("tile", None),
            P("tile", None, None),
            P(),
            P(),
            P(),
            P("tile", "blk"),
            P("tile", "blk"),
            P("blk", "tile"),
        ),
        out_specs=P("tile", "blk", None),
        check_vma=False,
    )
```

```python
import functools
import math

import jax
import jax.numpy as jnp
from jax import lax
from jax.experimental import pallas as pl
from jax.experimental.pallas import tpu as pltpu
from jax.sharding import PartitionSpec as P

X, YH = 4, 2
Z, YL, CORES = 8, 4, 2
HEAD_DIM = 64
CAP = 2
EPS = 1e-06
NEG = -1e30
FLOOR = -1e29
STATS = 16
SENDS, RECEIVES = 34, 55
F32, BF16 = jnp.float32, jnp.bfloat16
MESH = pl.DeviceIdType.MESH

NT = (((1,), (1,)), ((), ()))
NN = (((1,), (0,)), ((), ()))


def dot(a, b, dims=NN):
    return lax.dot_general(a, b, dims, preferred_element_type=F32)


def iota(shape, axis):
    return lax.broadcasted_iota(jnp.int32, shape, axis)


def as_column(row):
    n = row.shape[1]
    same = iota((n, n), 0) == iota((n, n), 1)
    return jnp.sum(jnp.where(same, row, 0), axis=1, keepdims=True)


def split3(value):
    high = value.astype(BF16).astype(F32)
    rest = value - high
    middle = rest.astype(BF16).astype(F32)
    return high, middle, rest - middle


def standardize(rows):
    centered = rows - jnp.mean(rows, axis=-1, keepdims=True)
    inverse = lax.rsqrt(jnp.mean(centered * centered, axis=-1, keepdims=True) + EPS)
    return centered * inverse, inverse


def kernel(
    len_hbm, q_hbm, k_hbm, v_hbm, pos_hbm, own_hbm, row_hbm, e_hbm, st_hbm,
    gain_hbm, bias_hbm, ls_hbm, wg_hbm, wu_hbm, wd_hbm,
    out_ref,
    len_ref, q_ref, k_ref, v_ref, pos_ref, own_ref, row_ref, e_ref, st_ref,
    gain_ref, bias_ref, ls_ref, wg_ref, wu_ref, wd_ref,
    qall, kmask, vt, mask, stat, ret, ret_in, ysend, ymine, yrecv,
    xs, spread, meta, meta_a, meta_b, combine, r1a, r1b, pa, pb, r2a, r2b, sums, cot, cot_sum, rs, rs_in, ry_send, ry_in,
    wpair, wout, wfull, efull, normed, fwd, hid, gu,
    load_sems, send_sems, recv_sems,
):
    blk, tile = lax.axis_index("blk"), lax.axis_index("tile")
    x, yh = blk // YH, blk % YH
    core = tile % CORES
    yl = (tile // CORES) % YL
    z = tile // (CORES * YL)
    lane = tile % (CORES * YL)
    side = CORES * YL

    tokens, width = k_ref.shape[1], k_ref.shape[2]
    samples = pos_ref.shape[1]
    heads_half = width // HEAD_DIM // 2
    half_rows = width // 2
    ff = wg_ref.shape[1]
    own = out_ref.shape[1]
    rows_all = st_ref.shape[1]
    dt = st_ref.shape[2]
    shard = e_ref.shape[0]
    scale = 1.0 / math.sqrt(HEAD_DIM) * math.log2(math.e)
    part = 3 * ff // 2

    def at(new_x=None, new_yh=None, new_z=None, new_yl=None, new_core=None):
        a = x if new_x is None else new_x
        b = yh if new_yh is None else new_yh
        c = z if new_z is None else new_z
        d = yl if new_yl is None else new_yl
        e = core if new_core is None else new_core
        return (a * YH + b, (c * YL + d) * CORES + e)

    def x_peer(d):
        return at(new_x=lax.rem(x + d, X))

    def z_peer(d):
        return at(new_z=lax.rem(z + d + Z, Z))

    def side_peer(d):
        other = lax.rem(lane + d, side)
        return (blk, z * side + other)

    def y_peer(d):
        place = lax.rem(yh * YL + yl + d + YH * YL, YH * YL)
        return at(new_yh=place // YL, new_yl=place % YL)

    partner = at(new_yh=1 - yh)
    sibling = at(new_core=1 - core)

    barrier = pltpu.get_barrier_semaphore()
    targets = [partner]
    targets += [x_peer(d) for d in range(1, X)]
    targets += [z_peer(d) for d in range(1, Z)]
    targets += [side_peer(d) for d in range(1, side)]
    targets += [y_peer(d) for d in (1, -1, 2, -2)]
    for target in targets:
        pl.semaphore_signal(barrier, inc=1, device_id=target, device_id_type=MESH)

    loads = {}
    for index, (name, source, target) in enumerate([
        ("pos", pos_hbm, pos_ref), ("q", q_hbm, q_ref), ("wg", wg_hbm, wg_ref),
        ("wu", wu_hbm, wu_ref), ("wd", wd_hbm, wd_ref), ("e", e_hbm, e_ref),
        ("len", len_hbm, len_ref), ("k", k_hbm, k_ref), ("v", v_hbm, v_ref),
        ("st", st_hbm, st_ref), ("gain", gain_hbm, gain_ref), ("bias", bias_hbm, bias_ref),
        ("own", own_hbm, own_ref), ("row", row_hbm, row_ref), ("ls", ls_hbm, ls_ref),
    ]):
        loads[name] = pltpu.make_async_copy(source, target, load_sems.at[index])
        loads[name].start()

    def loaded(*names):
        for name in names:
            loads.pop(name).wait()

    copies = []
    live, free, free_of, numbers = [], [], [], []

    def retire(until):
        while live and len(copies) - len(live) < until:
            copy, index = live.pop(0)
            copy.wait_send()
            free.append(index)

    def together(ref, open_end=False):
        return {"ref": ref, "open": open_end}

    def remote(src, dst, target, index, number):
        return pltpu.make_async_remote_copy(
            src_ref=src, dst_ref=dst,
            send_sem=send_sems.at[index], recv_sem=recv_sems.at[number],
            device_id=target, device_id_type=MESH,
        )

    def send(src, dst, target, among=None):
        if among is not None and "copy" in among:
            remote(src, dst, target, among["index"], among["number"]).start()
            return among["copy"]
        index = free.pop() if free else len(free_of)
        if index == len(free_of):
            free_of.append(index)
        number = len(numbers)
        numbers.append(number)
        copy = remote(src, dst, target, index, number)
        copy.start()
        if among is not None:
            ref = among["ref"]
            copy = remote(ref, ref, target, index, number)
            among.update(copy=copy, index=index, number=number)
        if among is None or not among["open"]:
            copies.append(copy)
            live.append((copy, index))
        return copy

    def take(among):
        among["copy"].wait_recv()
        if among["open"]:
            copies.append(among["copy"])
            live.append((among["copy"], among["index"]))

    loaded("pos", "q")
    chosen = (as_column(pos_ref[...]) == iota((samples, tokens), 1)).astype(F32).astype(BF16)
    my_rows = pl.ds(pl.multiple_of(x * samples, samples), samples)
    qall[yh, my_rows, :] = dot(chosen, q_ref[0]).astype(BF16)

    loaded("wg", "wu", "wd", "e")
    cut = ff // 2

    def fill(mine, first):
        if first:
            mine[:, 0:ff] = wg_ref[...]
            mine[:, ff:part] = wu_ref[:, 0:cut]
            mine[:, part:] = e_ref[:, 0:half_rows]
        else:
            mine[:, 0:cut] = wu_ref[:, cut:]
            mine[:, cut:part] = wd_ref[...]
            mine[:, part:] = e_ref[:, half_rows:]

    @pl.when(core == 0)
    def _():
        fill(wpair.at[0], True)
        fill(wout, False)

    @pl.when(core == 1)
    def _():
        fill(wpair.at[1], False)
        fill(wout, True)

    pl.semaphore_wait(barrier, len(targets))

    parts = [slice(0, half_rows), slice(half_rows, width)]
    q_y = []
    for part_of in parts:
        rows = qall.at[yh, my_rows, part_of]
        q_y.append(send(rows, rows, partner))
    w_pair = send(wout, wpair.at[core], sibling)
    three = pl.ds(0, (X - 1) * samples)
    q_near = together(qall.at[0, three])
    for d in range(1, X):
        send(qall.at[yh, my_rows], qall.at[yh, my_rows], x_peer(d), q_near)

    w_pair.wait_recv()
    whole = jnp.concatenate([wpair[0].astype(F32), wpair[1].astype(F32)], axis=0).astype(BF16)
    wfull[core, z, yl] = whole[:, 0:part]
    efull[core, z, yl] = whole[:, part:]

    turn = 1 - 2 * core

    def step_blocks(step):
        up, down = lax.rem(z - (step - 1) + Z, Z), lax.rem(z + (step - 1), Z)
        if step < Z // 2:
            return [(up, 1), (down, -1)]
        return [(lax.rem(z - turn * (step - 1) + Z, Z), turn)]

    def first_ring(step):
        groups = []
        for ref in (efull, wfull):
            blocks = step_blocks(step)
            groups.append(together(ref.at[core, 0:len(blocks), 0]))
            for block, way in blocks:
                place = ref.at[core, block, yl]
                send(place, place, z_peer(way), groups[-1])
        return groups

    def second_ring(step, d):
        blocks = step_blocks(step)
        group = together(wfull.at[core, 0:len(blocks), 0])
        for block, way in blocks:
            place = wfull.at[core, block, lax.rem(yl + d, YL)]
            send(place, place, z_peer(way), group)
        return group

    e_line = together(efull.at[core, :, 0:YL - 1], True)

    def e_along_y(block, way):
        place = efull.at[core, block, yl]
        for d in (1, -1, 2 * way):
            send(place, place, y_peer(d), e_line)

    def wait(sent):
        for copy in sent:
            copy.wait_recv()

    pass_on = together(wfull.at[core], True)

    def to_sibling(block):
        send(wfull.at[core, block], wfull.at[core, block], sibling, pass_on)

    def arrived_first(sent, step):
        for group in sent:
            take(group)
        following = None
        if step < Z // 2:
            following = first_ring(step + 1)
            e_along_y(lax.rem(z - step + Z, Z), 1)
            e_along_y(lax.rem(z + step, Z), -1)
        else:
            e_along_y(lax.rem(z + step, Z), 1)
        return following

    def arrived_second(sent, step):
        following = {}
        for d in sent:
            take(sent[d])
            if step < Z // 2:
                following[d] = second_ring(step + 1, d)
        if step < Z // 2:
            to_sibling(lax.rem(z - step + Z, Z))
        to_sibling(lax.rem(z + step, Z))
        return following

    ring = first_ring(1)

    loaded("len", "k", "v")
    positions = blk * tokens + iota((tokens, X * samples), 0)
    mask[...] = jnp.where(positions < len_ref[0], 0.0, NEG).astype(F32)
    vt[...] = v_ref[0].astype(F32).T.astype(BF16)
    keys = k_ref[0]
    even = iota((tokens, width), 1) % 128 < HEAD_DIM
    kmask[0] = jnp.where(even, keys, jnp.zeros_like(keys))
    kmask[1] = jnp.where(even, jnp.zeros_like(keys), keys)
    stat[...] = jnp.zeros_like(stat)

    loaded("st", "gain", "bias")
    xhat, unused = standardize(st_ref[0].astype(F32))
    gain = gain_ref[...].reshape(1, dt)
    normed[...] = (xhat * gain + bias_ref[...].reshape(1, dt)).astype(BF16)

    loaded("own", "row")
    slots = Z * side * CAP
    owner_row = own_ref[...]
    owner_col = as_column(owner_row)
    square = (samples, samples)
    earlier = (owner_col == owner_row) & (iota(square, 0) < iota(square, 1))
    rank = jnp.sum(jnp.where(earlier, 1, 0), axis=0, keepdims=True)
    slot_a = owner_row * CAP + rank
    slot_b = (owner_row % side) * (Z * CAP) + (owner_row // side) * CAP + rank
    for route, slot in enumerate((slot_a, slot_b)):
        hit = iota((slots, samples), 0) == slot
        table_row = jnp.sum(jnp.where(hit, row_ref[...] + 1, 0), axis=1, keepdims=True) - 1
        meta[route] = (table_row == iota((slots, 128), 1)).astype(F32).astype(BF16)
        hit = hit.astype(F32)
        spread[route] = jnp.concatenate([hit, jnp.zeros_like(hit)], axis=1).astype(BF16)
    group, count = side * CAP, Z * CAP

    def rows_at(index, size):
        return pl.ds(pl.multiple_of(index * size, size), size)

    def first_leg(source, along_z, along_side):
        sent = together(along_z.at[0:Z - 1]), together(along_side.at[0:side - 1])
        for d in range(1, Z):
            rows = rows_at(lax.rem(z + d, Z), group)
            send(source.at[0, rows], along_z.at[z], z_peer(d), sent[0])
        for d in range(1, side):
            rows = rows_at(lax.rem(lane + d, side), count)
            send(source.at[1, rows], along_side.at[lane], side_peer(d), sent[1])
        along_z[z] = source[0, rows_at(z, group), :]
        along_side[lane] = source[1, rows_at(lane, count), :]
        return sent

    meta_sent = first_leg(meta, meta_a, meta_b)

    retire(len(q_y))
    w_line = [
        send(
            wfull.at[core, z, yl], wfull.at[core, z, yl],
            at(new_yl=lax.rem(yl + d, YL)),
        )
        for d in range(1, YL)
    ]
    e_along_y(z, 1)
    ring = arrived_first(ring, 1)

    q_far = []
    for part_of, copy in zip(parts, q_y):
        copy.wait_recv()
        rows = qall.at[1 - yh, my_rows, part_of]
        q_far.append(together(qall.at[0, three, part_of]))
        for d in range(1, X):
            send(rows, rows, x_peer(d), q_far[-1])
    def pack(first, second):
        both = 2 * samples
        low = iota((first.shape[0], both), 1) < samples
        pieces = []
        for start in range(0, X * samples, both):
            a, b = first[:, start:start + both], second[:, start:start + both]
            pieces.append(jnp.where(low, a, pltpu.roll(b, samples, 1)))
            pieces.append(jnp.where(low, pltpu.roll(a, samples, 1), b))
        return pieces

    pairs = heads_half // 2
    kept_rows = pairs * HEAD_DIM

    def stats_of(top, total):
        return split3(top) + split3(total)[:2]

    def attend(group, half):
        for pair in range(pairs):
            mixed, tops, totals = [], [], []
            for head in (half * heads_half + pair, half * heads_half + pair + pairs):
                features = slice(head // 2 * 128, head // 2 * 128 + 128)
                scores = dot(kmask[head % 2, :, features], qall[group, :, features], NT)
                scores += mask[...]
                top = jnp.maximum(jnp.max(scores, axis=0, keepdims=True), FLOOR)
                weights = jnp.exp2((scores - top) * scale)
                tops.append(top)
                totals.append(jnp.sum(weights, axis=0, keepdims=True))
                mine = slice(head * HEAD_DIM, head * HEAD_DIM + HEAD_DIM)
                mixed.append(dot(vt[mine, :], weights.astype(BF16)))
            rows = slice(pair * HEAD_DIM, pair * HEAD_DIM + HEAD_DIM)
            packed_tops, packed_totals = pack(*tops), pack(*totals)
            for place, piece in enumerate(pack(*mixed)):
                ret[half, group, place, rows, :] = piece.astype(BF16)
                rows_in = stats_of(packed_tops[place], packed_totals[place])
                for kind, row in enumerate(rows_in):
                    at_row = kind * pairs + pair
                    stat[place, at_row:at_row + 1, :] = row
        for place in range(X):
            ret[half, group, place, kept_rows:, :] = stat[place].astype(BF16)

    def back_to_x_peers(group, half):
        sent = together(ret_in.at[half, group])
        for d in range(1, X):
            place = lax.rem(x + d, X)
            send(ret.at[half, group, place], ret_in.at[half, group, d - 1], x_peer(d), sent)
        return sent

    def merge(terms):
        stats = [term[kept_rows:] for term in terms]

        def kind(s, index):
            return s[index * pairs:(index + 1) * pairs]

        tops = [kind(s, 0) + kind(s, 1) + kind(s, 2) for s in stats]
        top = functools.reduce(jnp.maximum, tops)
        factors = [jnp.exp2((t - top) * scale) for t in tops]
        total = sum(f * (kind(s, 3) + kind(s, 4)) for f, s in zip(factors, stats))
        rows = []
        for head in range(pairs):
            here = slice(head * HEAD_DIM, head * HEAD_DIM + HEAD_DIM)
            rows.append(sum(f[head:head + 1] * t[here] for f, t in zip(factors, terms)))
        return rows, top, total

    def merged(group, half, target):
        rows, top, total = merge(
            [ret[half, group, x].astype(F32)]
            + [ret_in[half, group, d].astype(F32) for d in range(X - 1)]
        )
        for head in range(pairs):
            target[half, head * HEAD_DIM:(head + 1) * HEAD_DIM, :] = rows[head].astype(
                target.dtype
            )
        for index, pieces in enumerate(stats_of(top, total)):
            stat[0, index * pairs:(index + 1) * pairs, :] = pieces
        target[half, kept_rows:, :] = stat[0].astype(target.dtype)

    take(q_near)
    for half in range(2):
        attend(yh, half)
    if Z >= 4:
        ring = arrived_first(ring, 2)

    ring_two = {}
    for d in range(1, YL):
        w_line[YL - 1 - d].wait_recv()
        ring_two[d] = second_ring(1, d)
    to_sibling(z)

    back_far = []
    for half in range(2):
        take(q_far[half])
        attend(1 - yh, half)
        back_far.append(back_to_x_peers(1 - yh, half))
    for step in range(3, Z // 2):
        ring = arrived_first(ring, step)
    begun = len(copies)
    if Z >= 4:
        ring_two = arrived_second(ring_two, 1)

    back_y = []
    for half in range(2):
        take(back_far[half])
        merged(1 - yh, half, ysend)
        back_y.append(send(ysend.at[half], yrecv.at[half], partner))
    back_near = [back_to_x_peers(yh, half) for half in range(2)]

    if Z >= 4:
        arrived_first(ring, Z // 2)
    if Z >= 6:
        ring_two = arrived_second(ring_two, 2)
    for route, came, others in ((0, meta_a, side), (1, meta_b, Z)):
        take(meta_sent[route])
        rows = came[...].reshape(slots, 128).astype(F32).T[0:own]
        rows = jnp.concatenate([rows] * others, axis=0)
        shape = (others * own, slots)
        same = iota(shape, 0) // own == (iota(shape, 1) // CAP) % others
        combine[route, 0:others * own, :] = jnp.where(same, rows, 0.0).astype(BF16)

    for half in range(2):
        take(back_near[half])
        merged(yh, half, ymine)
    retire(begun)
    for half in range(2):
        back_y[half].wait_recv()
        rows, unused, total = merge([ymine[half], yrecv[half].astype(F32)])
        picked = jnp.concatenate([rows[h] / total[h:h + 1] for h in range(pairs)], axis=0)
        picked = jnp.concatenate([picked, pltpu.roll(picked, samples, 1)], axis=0)
        xs[half] = dot(spread[half], picked.astype(BF16), NT).astype(BF16)
    leg_one = first_leg(xs, r1a, r1b)
    for step in range(3, Z // 2):
        ring_two = arrived_second(ring_two, step)

    take(leg_one[0])
    pa[...] = dot(combine[0, 0:side * own], r1a[...].reshape(slots, half_rows)).astype(BF16)
    leg_two = [together(r2a.at[0:side - 1]), together(r2b.at[0:Z - 1])]
    for d in range(1, side):
        rows = rows_at(lax.rem(lane + d, side), own)
        send(pa.at[rows], r2a.at[lane], side_peer(d), leg_two[0])
    r2a[lane] = pa[rows_at(lane, own), :]
    take(leg_one[1])
    pb[...] = dot(combine[1, 0:Z * own], r1b[...].reshape(slots, half_rows)).astype(BF16)
    for d in range(1, Z):
        send(pb.at[rows_at(lax.rem(z + d, Z), own)], r2b.at[z], z_peer(d), leg_two[1])
    r2b[z] = pb[rows_at(z, own), :]
    if Z < 4:
        arrived_first(ring, 1)
    take(e_line)
    e_sibling = send(efull.at[core], efull.at[core], sibling)
    arrived_second(ring_two, Z // 2)
    step_rows = 2 * YL * CORES * shard
    steps = dt // step_rows

    def block_of(ref, half, i, columns):
        return ref[half, pl.ds(2 * i, 2), :, :, columns].reshape(
            step_rows, columns.stop - columns.start
        )

    def columns_of(i):
        return pl.ds(pl.multiple_of(i * step_rows, step_rows), step_rows)

    for group_of in leg_two:
        take(group_of)
    my_table = pl.ds(pl.multiple_of(yh * own, own), own)
    sums[x, my_table, 0:half_rows] = jnp.sum(r2a[...].astype(F32), axis=0).astype(BF16)
    sums[x, my_table, half_rows:] = jnp.sum(r2b[...].astype(F32), axis=0).astype(BF16)
    begun = len(copies)
    sums_y = send(sums.at[x, my_table], sums.at[x, my_table], partner)
    sums_x = [together(sums.at[0:X - 1, 0:own]) for unused in range(2)]
    for d in range(1, X):
        send(sums.at[x, my_table], sums.at[x, my_table], x_peer(d), sums_x[0])

    take(pass_on)
    fwd[...] = jnp.zeros_like(fwd)

    def forward(i, carry):
        rows = normed[:, columns_of(i)]
        fwd[:, 0:part] += dot(rows, block_of(wfull, 0, i, slice(0, part)))
        fwd[:, part:] += dot(rows, block_of(wfull, 1, i, slice(0, cut)))
        return carry

    lax.fori_loop(0, steps, forward, 0)

    retire(begun)
    sums_y.wait_recv()
    other_table = pl.ds(pl.multiple_of((1 - yh) * own, own), own)
    for d in range(1, X):
        send(sums.at[x, other_table], sums.at[x, other_table], x_peer(d), sums_x[1])
    e_sibling.wait_recv()
    for group_of in sums_x:
        take(group_of)

    def project(i, carry):
        grads, every = sums[...].reshape(rows_all, width), slice(0, half_rows)
        terms = dot(grads[:, 0:half_rows], block_of(efull, 0, i, every), NT)
        terms += dot(grads[:, half_rows:], block_of(efull, 1, i, every), NT)
        cot[:, :, columns_of(i)] = terms.astype(BF16).reshape(X, YH * own, step_rows)
        return carry

    lax.fori_loop(0, steps, project, 0)

    loaded("ls")
    layer_scale = ls_ref[...].reshape(1, dt)
    scaled = (cot[...].reshape(rows_all, dt).astype(F32) * layer_scale).astype(BF16)
    normed[...] = scaled
    hid[...] = jnp.zeros_like(hid)

    def hidden(i, carry):
        hid[...] += dot(normed[:, columns_of(i)], block_of(wfull, 1, i, slice(cut, part)))
        return carry

    lax.fori_loop(0, steps, hidden, 0)
    gate, up, hidden_cot = fwd[:, 0:ff], fwd[:, ff:], hid[...]
    sigmoid = jax.nn.sigmoid(gate)
    gu[:, 0:ff] = (hidden_cot * up * sigmoid * (1.0 + gate * (1.0 - sigmoid))).astype(BF16)
    gu[:, ff:] = (hidden_cot * gate * sigmoid).astype(BF16)

    def backward(i, carry):
        terms = dot(gu[:, 0:part], block_of(wfull, 0, i, slice(0, part)), NT)
        terms += dot(gu[:, part:], block_of(wfull, 1, i, slice(0, cut)), NT)
        rs[:, :, columns_of(i)] = terms.astype(BF16).reshape(X, YH * own, step_rows)
        return carry

    sum_x, sum_y, portions = [], [], 4
    chunks = [slice(c * dt // portions, (c + 1) * dt // portions) for c in range(portions)]
    for c, chunk in enumerate(chunks):
        lax.fori_loop(c * steps // portions, (c + 1) * steps // portions, backward, 0)
        sum_x.append(together(rs_in.at[:, :, chunk]))
        for d in range(1, X):
            other = rs.at[lax.rem(x + d, X), :, chunk]
            send(other, rs_in.at[d - 1, :, chunk], x_peer(d), sum_x[c])
    xhat, inverse = standardize(
        st_ref[0, pl.ds(pl.multiple_of(blk * own, own), own), :].astype(F32)
    )
    for c, chunk in enumerate(chunks):
        take(sum_x[c])
        partial = rs[x, :, chunk].astype(F32)
        for d in range(X - 1):
            partial += rs_in[d, :, chunk].astype(F32)
        cot_sum[:, chunk] = partial
        ry_send[:, chunk] = cot_sum[other_table, chunk].astype(BF16)
        sum_y.append(send(ry_send.at[:, chunk], ry_in.at[:, chunk], partner))
    base = cot[x, my_table, :].astype(F32)
    retire(len(copies) - len(sum_y))
    wait(sum_y)
    grads_in = (cot_sum[my_table, :] + ry_in[...].astype(F32)) * gain
    result = base + inverse * (
        grads_in
        - jnp.mean(grads_in, axis=-1, keepdims=True)
        - xhat * jnp.mean(grads_in * xhat, axis=-1, keepdims=True)
    )
    out_ref[0] = result.astype(BF16)

    retire(len(copies))


def local(
    queries, key_rows, values, slide_lens, sample_pos, owner_ids, owner_rows, embed_proj,
    tile_states, layernorm_gain, layernorm_bias, layer_scale, w_gate, w_up, w_down,
):
    tokens, width = key_rows.shape[1:]
    samples = sample_pos.shape[1]
    rows_all, dt = tile_states.shape[1:]
    shard, ff = w_gate.shape
    own = rows_all // (X * YH)
    both = 2 * samples
    half = width // 2
    part_rows = half // 2 + STATS
    side = CORES * YL
    slots = Z * side * CAP
    part = 3 * ff // 2
    vmem = pltpu.VMEM
    operands = (
        slide_lens, queries, key_rows, values, sample_pos, owner_ids[:, :, 0], owner_rows,
        embed_proj, tile_states, layernorm_gain, layernorm_bias, layer_scale, w_gate, w_up,
        w_down.T,
    )
    scratch = [pltpu.SMEM(slide_lens.shape, jnp.int32)]
    scratch += [vmem(operand.shape, operand.dtype) for operand in operands[1:]]
    scratch += [
        vmem((YH, X * samples, width), BF16),
        vmem((2, tokens, width), BF16),
        vmem((width, tokens), BF16),
        vmem((tokens, X * samples), F32),
        vmem((X, STATS, both), F32),
        vmem((2, YH, X, part_rows, both), BF16),
        vmem((2, YH, X - 1, part_rows, both), BF16),
        vmem((2, part_rows, both), BF16),
        vmem((2, part_rows, both), F32),
        vmem((2, part_rows, both), BF16),
        vmem((2, slots, half), BF16),
        vmem((2, slots, both), BF16),
        vmem((2, slots, 128), BF16),
        vmem((Z, side * CAP, 128), BF16),
        vmem((side, Z * CAP, 128), BF16),
        vmem((2, side * own, slots), BF16),
        vmem((Z, side * CAP, half), BF16),
        vmem((side, Z * CAP, half), BF16),
        vmem((side * own, half), BF16),
        vmem((Z * own, half), BF16),
        vmem((side, own, half), BF16),
        vmem((Z, own, half), BF16),
        vmem((X, YH * own, width), BF16),
        vmem((X, YH * own, dt), BF16),
        vmem((YH * own, dt), F32),
        vmem((X, YH * own, dt), BF16),
        vmem((X - 1, YH * own, dt), BF16),
        vmem((own, dt), BF16),
        vmem((own, dt), BF16),
        vmem((CORES, shard, part + width // 2), BF16),
        vmem((shard, part + width // 2), BF16),
        vmem((2, Z, YL, CORES * shard, part), BF16),
        vmem((2, Z, YL, CORES * shard, width // 2), BF16),
        vmem((rows_all, dt), BF16),
        vmem((rows_all, 2 * ff), F32),
        vmem((rows_all, ff), F32),
        vmem((rows_all, 2 * ff), BF16),
        pltpu.SemaphoreType.DMA((len(operands),)),
        pltpu.SemaphoreType.DMA((SENDS,)),
        pltpu.SemaphoreType.DMA((RECEIVES,)),
    ]
    return pl.pallas_call(
        kernel,
        out_shape=jax.ShapeDtypeStruct((1, own, dt), BF16),
        in_specs=[pl.BlockSpec(memory_space=pl.ANY)] * len(operands),
        out_specs=pl.BlockSpec(memory_space=pltpu.VMEM),
        scratch_shapes=scratch,
        compiler_params=pltpu.CompilerParams(
            collective_id=0, has_side_effects=True, vmem_limit_bytes=60 * 1024 * 1024
        ),
    )(*operands)


def solution(mesh):
    return jax.shard_map(
        local,
        mesh=mesh,
        in_specs=(
            P("tile", "blk", None),
            P("tile", "blk", None),
            P("tile", "blk", None),
            P("tile"),
            P("tile", "blk"),
            P("tile", "blk", None),
            P("tile", "blk"),
            P("tile", None),
            P("tile", None, None),
            P(),
            P(),
            P(),
            P("tile", "blk"),
            P("tile", "blk"),
            P("blk", "tile"),
        ),
        out_specs=P("tile", "blk", None),
        check_vma=False,
    )
```
